512 devices in a mesh: frame: 4 (over y), vox: 128 (over x, z, core).
Axes of the slice: x: 4, y: 4, z: 16, core: 2. Of those that a mesh axis runs over, the one named last changes fastest.
Arguments:
- pool: bfloat16 [2048, 131072], P('frame', 'vox'), may hold values from -6 to 6
- dictionary: bfloat16 [1024, 131072], P(None, 'vox'), may hold values from -0.03314563 to 0.03314563
- support: int32 [1024, 1024], P(None, 'vox'), may hold values from 0 to 1, as said below
- pick: int32 [1024], P('frame'), may hold values from 0 to 511
Outputs:
- codes: bfloat16 [1024, 1024], P('frame')
- gradient: float32 [1024, 131072], P('frame', 'vox')
The draws below stay inside these ranges and needn't reach their ends.
Inputs may be any that keep to these rules, and one draw needn't show every extreme that they name: Every mode has at least one voxel block in its support.
All inputs are finite; a program needn't handle non-finite values.
Results may differ from the reference program's by a relative error of at most 0.015.
Values may be sent and summed in bfloat16 or wider, within the bound.
A program may use at most 64 MiB of HBM per device.

```python
import jax
import jax.numpy as jnp
from jax import lax

MODES = 1024
BLOCK = 128
FRAME_DEV = 256
BLOCKS = 1024
VOXELS = 131072
FRAMES = 1024
POOL = 2048
N_FRAME = 4


def draw_support(key, part):
    values = jax.random.randint(key, (MODES, BLOCKS), 0, 4)
    forced = jnp.arange(BLOCKS)[None, :] == jnp.arange(MODES)[:, None] % BLOCKS
    return jnp.where((values != 0) | forced, 1, 0).astype(jnp.int32)


def draw_dictionary(key, part):
    key_base = jax.random.fold_in(key, 11)
    key_mode = jax.random.fold_in(key, 12)
    key_block = jax.random.fold_in(key, 13)
    base = jnp.clip(jax.random.normal(key_base, (MODES, VOXELS), jnp.float32), -4.0, 4.0)
    mode_lo, mode_hi = (0.55, 1.8)
    mode_level = jnp.exp(jax.random.uniform(key_mode, (MODES, 1), jnp.float32, jnp.log(mode_lo), jnp.log(mode_hi)))
    block_level = jnp.exp(jax.random.uniform(key_block, (MODES, BLOCKS), jnp.float32, jnp.log(0.6), jnp.log(1.6)))
    block_wide = jnp.repeat(block_level, BLOCK, axis=1)
    scale = 1.0 / jnp.sqrt(jnp.float32(VOXELS))
    return (base * mode_level * block_wide * scale).astype(jnp.bfloat16)


def touch_ends(entries, rng, low, largest):
    dims = entries.shape
    spot = [jax.random.randint(jax.random.fold_in(rng, axis), (), 0, dims[axis]) for axis in range(len(dims))]
    entries = entries.at[tuple(spot)].set(low)
    longest = dims.index(max(dims))
    spot[longest] = (spot[longest] + 1) % dims[longest]
    return entries.at[tuple(spot)].set(largest)


def level_of(stream_key, dims, pieces, least, largest):
    def one(axis_at, parts):
        steps = jax.random.uniform(jax.random.fold_in(jax.random.fold_in(stream_key, 6), axis_at), (parts,), jnp.float32, least / len(pieces), largest / len(pieces))
        return jnp.repeat(jnp.exp(steps), dims[axis_at] // parts).reshape((-1,) + (1,) * (len(dims) - axis_at - 1))

    factor_of = one(*pieces[0])
    for cut in pieces[1:]:
        factor_of = factor_of * one(*cut)
    return factor_of


def scatter_about(stream_key, dims, width, most, shards=(), kind=jnp.bfloat16):
    result = width * jax.random.normal(stream_key, dims, jnp.float32)
    if shards:
        result = result * level_of(stream_key, dims, shards, -0.22, 0.18)
    return jnp.clip(result, -most, most).astype(kind)


def setup_inputs(seed: int = 0) -> dict:
    seeds = jax.random.split(jax.random.key(seed), 5)
    pool = scatter_about(seeds[0], (POOL, VOXELS), 1.0, 6.0, ((0, 4), (1, 128)))
    dictionary = draw_dictionary(jax.random.fold_in(seeds[4], 71), 0)
    support = draw_support(jax.random.fold_in(seeds[4], 71), 0)
    pick = touch_ends(jax.random.randint(seeds[3], (FRAMES,), 0, 2 * FRAME_DEV), jax.random.fold_in(seeds[3], 1), 0, (2 * FRAME_DEV) - 1).astype(jnp.int32)
    return dict(pool=pool, dictionary=dictionary, support=support, pick=pick)


def shrink(value, limit):
    return jnp.sign(value) * jnp.maximum(jnp.abs(value) - limit, 0.0)


def reference(pool, dictionary, support, pick):
    rows = (jnp.arange(FRAMES, dtype=jnp.int32) // FRAME_DEV) * (2 * FRAME_DEV) + pick
    batch = pool[rows]
    keep = jnp.repeat(support, BLOCK, axis=1).astype(jnp.bfloat16)
    masked = dictionary * keep
    corr = jnp.dot(batch, masked.T, preferred_element_type=jnp.float32)
    energy = jnp.sum(jnp.square(masked.astype(jnp.float32)), axis=1)
    step = 1.0 / (energy + 1e-5)
    first = shrink(corr * step, 0.3 * step).astype(jnp.bfloat16)
    resid = (jnp.dot(first, masked, preferred_element_type=jnp.float32) - batch.astype(jnp.float32)).astype(jnp.bfloat16)
    push = jnp.dot(resid, masked.T, preferred_element_type=jnp.float32)
    codes = shrink(first.astype(jnp.float32) - step * push, 0.3 * step).astype(jnp.bfloat16)
    error = (jnp.dot(codes, masked, preferred_element_type=jnp.float32) - batch.astype(jnp.float32)).astype(jnp.bfloat16)
    code_groups = codes.reshape(N_FRAME, FRAME_DEV, MODES)
    error_groups = error.reshape(N_FRAME, FRAME_DEV, VOXELS)

    def add_group(total, pair):
        part = jnp.dot(pair[0].T, pair[1], preferred_element_type=jnp.float32).astype(jnp.bfloat16)
        return total + part.astype(jnp.float32), None

    total, _ = lax.scan(add_group, jnp.zeros((MODES, VOXELS), jnp.float32), (code_groups, error_groups))
    gradient = keep.astype(jnp.float32) * total / FRAMES
    return codes, gradient
```

```python
import jax
import jax.numpy as jnp
from jax import lax
from jax.experimental import pallas as pl
from jax.experimental.pallas import tpu as pltpu
from jax.sharding import PartitionSpec as P

MESH = pl.DeviceIdType.MESH
NX, NY, NZ = 4, 4, 16
FAR = (8, 7, 9, 6, 10, 5, 11, 4, 12, 3, 13, 2, 14, 1, 15, 0)
OFFS = (2, 1, 3)
PLANE = tuple((i, j) for i in (2, 1, 3, 0) for j in (2, 1, 3, 0) if i or j)
BF, F32 = jnp.bfloat16, jnp.float32


def shrink(value, limit):
    return jnp.where(value < 0, -1.0, 1.0) * jnp.maximum(jnp.abs(value) - limit, 0.0)


def mm_t(left, right):
    return lax.dot_general(left, right, (((1,), (1,)), ((), ())), preferred_element_type=F32)


def mm_0(left, right):
    return lax.dot_general(left, right, (((0,), (0,)), ((), ())), preferred_element_type=F32)


def column(row):
    return jnp.transpose(jnp.broadcast_to(row, (128, 128)))


def kernel(
    pool, dico, supt, pick, codes_out, grad_out,
    masked, batch, psend, pown, precv, xsend, xrecv, zsend, zrecv, zown, zall,
    e_own, e_core, e_x, e_xr, e_z, e_zr, e_step, fall, gmat, call, error,
    s_b, r_b, s_p, r_p, s_ec, r_ec, s_ex, r_ex, s_ez, r_ez, s_x, r_x, s_z, r_z, s_a, r_a,
    s_f, r_f, s_fc, r_fc, s_g, r_g, s_c, r_c, s_cc, r_cc,
):
    y, v = lax.axis_index("frame"), lax.axis_index("vox")
    x, z, c = v // 32, (v // 2) % NZ, v % 2

    def dev(xx, yy, zz, cc):
        return (yy, (xx * NZ + zz) * 2 + cc)

    partner = dev(x, y, z, 1 - c)
    xs = [(x + i) % NX for i in OFFS]
    ys = [(y + i) % NY for i in OFFS]
    zs = [(z + o) % NZ for o in FAR]
    xpeer = [dev(xx, y, z, c) for xx in xs]
    ypeer = [dev(x, yy, z, c) for yy in ys]
    zpeer = [dev(x, y, zz, c) for zz in zs[:15]]
    plane = [((x + i) % NX, (y + j) % NY) for i, j in PLANE]
    ppeer = [dev(xx, yy, z, c) for xx, yy in plane]
    sent = []

    def send(src, dst, ssem, rsem, to):
        copy = pltpu.make_async_remote_copy(
            src_ref=src, dst_ref=dst, send_sem=ssem, recv_sem=rsem, device_id=to, device_id_type=MESH
        )
        copy.start()
        sent.append(copy)
        return copy

    barrier = pltpu.get_barrier_semaphore()
    everyone = [partner] + zpeer + ppeer
    for to in everyone:
        pl.semaphore_signal(barrier, inc=1, device_id=to, device_id_type=MESH)

    lane = lax.broadcasted_iota(jnp.int32, (128, 128), 1)
    mine = pl.multiple_of(y * 256, 256)
    for r in range(2):
        rows = column(pick[:, 128 * r : 128 * (r + 1)])
        hot = jnp.concatenate([(rows == lane + 128 * j).astype(F32).astype(BF) for j in range(4)], axis=1)
        batch[pl.ds(pl.multiple_of(y * 256 + 128 * r, 128), 128), :] = jnp.dot(
            hot, pool[...], preferred_element_type=F32
        ).astype(BF)

    block_of = lax.broadcasted_iota(jnp.int32, (8, 1024), 1) // 128
    spread = (block_of == lax.broadcasted_iota(jnp.int32, (8, 1024), 0)).astype(F32).astype(BF)

    def keep_rows(start, count):
        return mm_0(supt[:, pl.ds(start, count)].astype(F32).astype(BF), spread)

    @pl.loop(0, 8)
    def _(j):
        rows = pl.multiple_of(j * 128, 128)
        kept = dico[pl.ds(rows, 128), :] * keep_rows(rows, 128).astype(BF)
        masked[pl.ds(rows, 128), :] = kept
        wide = kept.astype(F32)
        part = jnp.zeros((128, 128), F32)
        for b in range(8):
            piece = wide[:, 128 * b : 128 * (b + 1)]
            part += piece * piece
        e_own[pl.ds(j, 1), :] = jnp.sum(jnp.transpose(part), axis=0, keepdims=True)

    pl.semaphore_wait(barrier, len(everyone))
    own_batch = batch.at[pl.ds(mine, 256), :]
    b_copies = [send(own_batch, own_batch, s_b.at[k], r_b.at[k], ypeer[k]) for k in range(3)]
    ec = send(e_own, e_core, s_ec, r_ec, partner)

    def products(half, out, kind):
        rows = pl.ds(pl.multiple_of(half * 512, 512), 512)
        right = (batch[pl.ds(mine, 256), :], masked[pl.ds(mine, 256), :])
        for g in range(2):
            value = mm_t(masked[rows, :], right[g]).astype(kind)
            for xx in range(4):
                for zz in range(16):
                    top = xx * 128 + 16 * (zz // 2)
                    left = 128 * (zz % 2)
                    out[xx * 16 + zz, 16 * g : 16 * (g + 1), :] = value[top : top + 16, left : left + 128]

    products(1 - c, psend, BF)
    pc = send(psend, precv, s_p, r_p, partner)
    ec.wait_recv()
    e_x[...] = e_own[...] + e_core[...]
    ex = [send(e_x, e_xr.at[k], s_ex.at[k], r_ex.at[k], xpeer[k]) for k in range(3)]
    products(c, pown, F32)

    pc.wait_recv()
    xc = []
    for j in range(4):
        for k in range(3):
            for q in range(4):
                t = xs[k] * 16 + zs[4 * j + q]
                xsend[k, 4 * j + q] = (pown[t] + precv[t].astype(F32)).astype(BF)
            piece = pl.ds(4 * j, 4)
            xc.append(send(xsend.at[k, piece], xrecv.at[k, piece], s_x.at[k, j], r_x.at[k, j], xpeer[k]))
    for k in range(3):
        ex[k].wait_recv()
    e_z[...] = e_x[...] + e_xr[0] + e_xr[1] + e_xr[2]
    ez = [send(e_z, e_zr.at[n], s_ez.at[n], r_ez.at[n], zpeer[n]) for n in range(15)]

    zc = []
    for j in range(4):
        for k in range(3):
            xc[3 * j + k].wait_recv()
        for q in range(4):
            n = 4 * j + q
            t = x * 16 + zs[n]
            total = pown[t] + precv[t].astype(F32)
            for k in range(3):
                total += xrecv[k, n].astype(F32)
            if n < 15:
                zsend[n] = total.astype(BF)
                zc.append(send(zsend.at[n], zrecv.at[n], s_z.at[n], r_z.at[n], zpeer[n]))
            else:
                zown[...] = total
    for n in range(15):
        ez[n].wait_recv()
    energy = e_z[...]
    for n in range(15):
        energy += e_zr[n]
    e_step[...] = 1.0 / (energy + 1e-05)
    total = zown[...]
    for n in reversed(range(15)):
        zc[n].wait_recv()
        total += zrecv[n].astype(F32)
    zall[z] = total.astype(BF)
    za = [send(zall.at[z], zall.at[z], s_a.at[n], r_a.at[n], zpeer[n]) for n in range(15)]

    block = c * 4 + x
    step = column(e_step[pl.ds(block, 1), :])
    step = jnp.concatenate([step, step], axis=1)
    limit = 0.3 * step
    for n in range(15):
        za[n].wait_recv()

    def own_part(g):
        sides = [jnp.concatenate([zall[2 * r + h, 16 * g : 16 * (g + 1), :] for r in range(8)], axis=0) for h in range(2)]
        return jnp.concatenate(sides, axis=1)

    gmat[y] = own_part(1)
    gc = [send(gmat.at[y], gmat.at[y], s_g.at[k], r_g.at[k], ypeer[k]) for k in range(3)]
    corr = own_part(0).astype(F32)
    first = shrink(corr * step, limit).astype(BF)
    fall[block] = first
    fx = [send(fall.at[block], fall.at[block], s_f.at[k], r_f.at[k], xpeer[k]) for k in range(3)]
    fc = [send(fall.at[block], fall.at[block], s_fc.at[3], r_fc.at[3], partner)]
    for k in range(3):
        fx[k].wait_recv()
        came = c * 4 + (x + NX - OFFS[k]) % NX
        fc.append(send(fall.at[came], fall.at[came], s_fc.at[k], r_fc.at[k], partner))
    for copy in gc + fc:
        copy.wait_recv()
    push = -corr
    for g in range(4):
        push += jnp.dot(gmat[g], jnp.concatenate([fall[2 * g], fall[2 * g + 1]], axis=0), preferred_element_type=F32)
    codes = shrink(first.astype(F32) - step * push, limit)
    call[block, pl.ds(mine, 256), :] = jnp.transpose(codes).astype(BF)

    def slot(b, yy):
        return call.at[b, pl.ds(pl.multiple_of(yy * 256, 256), 256), :]

    own_slot = slot(block, y)
    cx = [send(own_slot, own_slot, s_c.at[k], r_c.at[k], ppeer[k]) for k in range(15)]
    cc = [send(own_slot, own_slot, s_cc.at[15], r_cc.at[15], partner)]

    order = (0, 1, 3, 2)
    for turn, j in enumerate(order):
        yy = (y + NY - j) % NY
        here = [k for k in range(15) if PLANE[k][1] == j]
        waits = list(cc) if j == 0 else []
        for k in here:
            cx[k].wait_recv()
            came = slot(c * 4 + (x + NX - PLANE[k][0]) % NX, yy)
            waits.append(send(came, came, s_cc.at[k], r_cc.at[k], partner))
        for copy in waits:
            copy.wait_recv()
        if j:
            b_copies[OFFS.index(j)].wait_recv()
        rows = pl.ds(pl.multiple_of(yy * 256, 256), 256)
        group = jnp.concatenate([call[b, rows, :] for b in range(8)], axis=1)
        if j == 0:
            codes_out[...] = group
        own_modes = jnp.concatenate([call[2 * y, rows, :], call[2 * y + 1, rows, :]], axis=1)
        for n in range(4):
            cols = slice(256 * n, 256 * (n + 1))
            rest = jnp.dot(group, masked[:, cols], preferred_element_type=F32) - batch[rows, cols].astype(F32)
            part = mm_0(own_modes, rest.astype(BF))
            if turn == 0:
                grad_out[:, cols] = part
            elif turn < 3:
                grad_out[:, cols] += part
            else:
                error[:, cols] = grad_out[:, cols] + part
    grad_out[...] = error[...] * keep_rows(mine, 256) * (1.0 / 1024)
    for copy in sent:
        copy.wait_send()


def body(pool, dictionary, support, pick):
    dma = pltpu.SemaphoreType.DMA
    sems = []
    for shape in ((3,), (), (), (3,), (15,), (3, 4), (15,), (15,), (3,), (4,), (3,), (15,), (16,)):
        sems += [dma(shape), dma(shape)]
    vmem = pl.BlockSpec(memory_space=pltpu.VMEM)
    return pl.pallas_call(
        kernel,
        out_shape=(jax.ShapeDtypeStruct((256, 1024), BF), jax.ShapeDtypeStruct((256, 1024), F32)),
        in_specs=[vmem] * 4,
        out_specs=(vmem, vmem),
        scratch_shapes=[
            pltpu.VMEM((1024, 1024), BF),
            pltpu.VMEM((1024, 1024), BF),
            pltpu.VMEM((64, 32, 128), BF),
            pltpu.VMEM((64, 32, 128), F32),
            pltpu.VMEM((64, 32, 128), BF),
            pltpu.VMEM((3, 16, 32, 128), BF),
            pltpu.VMEM((3, 16, 32, 128), BF),
            pltpu.VMEM((15, 32, 128), BF),
            pltpu.VMEM((15, 32, 128), BF),
            pltpu.VMEM((32, 128), F32),
            pltpu.VMEM((16, 32, 128), BF),
            pltpu.VMEM((8, 128), F32),
            pltpu.VMEM((8, 128), F32),
            pltpu.VMEM((8, 128), F32),
            pltpu.VMEM((3, 8, 128), F32),
            pltpu.VMEM((8, 128), F32),
            pltpu.VMEM((15, 8, 128), F32),
            pltpu.VMEM((8, 128), F32),
            pltpu.VMEM((8, 128, 256), BF),
            pltpu.VMEM((4, 128, 256), BF),
            pltpu.VMEM((8, 1024, 128), BF),
            pltpu.VMEM((256, 1024), F32),
        ]
        + sems,
        compiler_params=pltpu.CompilerParams(
            collective_id=0, has_side_effects=True, vmem_limit_bytes=56 * 1024 * 1024
        ),
        cost_estimate=pl.CostEstimate(flops=6 * 10**9, bytes_accessed=6 * 2**20, transcendentals=0),
    )(pool, dictionary, jnp.transpose(support), jnp.reshape(pick, (1, 256)))


def solution(mesh):
    placed = (P("frame", "vox"), P(None, "vox"), P(None, "vox"), P("frame"))
    return jax.shard_map(
        body,
        mesh=mesh,
        in_specs=placed,
        out_specs=(P("frame", None), P("frame", "vox")),
        check_vma=False,
    )
```

```python
import jax
import jax.numpy as jnp
from jax import lax
from jax.experimental import pallas as pl
from jax.experimental.pallas import tpu as pltpu
from jax.sharding import PartitionSpec as P

MESH = pl.DeviceIdType.MESH
NX, NY, NZ = 4, 4, 16
FAR = (8, 7, 9, 6, 10, 5, 11, 4, 12, 3, 13, 2, 14, 1, 15, 0)
OFFS = (2, 1, 3)
SPLIT = 2
BF, F32 = jnp.bfloat16, jnp.float32


def shrink(value, limit):
    return jnp.where(value < 0, -1.0, 1.0) * jnp.maximum(jnp.abs(value) - limit, 0.0)


def mm_t(left, right):
    return lax.dot_general(left, right, (((1,), (1,)), ((), ())), preferred_element_type=F32)


def mm_0(left, right):
    return lax.dot_general(left, right, (((0,), (0,)), ((), ())), preferred_element_type=F32)


def column(row):
    return jnp.transpose(jnp.broadcast_to(row, (128, 128)))


def spread():
    block_of = lax.broadcasted_iota(jnp.int32, (8, 1024), 1) // 128
    return (block_of == lax.broadcasted_iota(jnp.int32, (8, 1024), 0)).astype(F32).astype(BF)


def gather(
    pool_in, dico_in, supt, pick, call, batch, masked,
    pool, dico, psend, pown, precv, xsend, xrecv, zsend, zrecv, zown, zall,
    e_own, e_core, e_x, e_xr, e_z, e_zr, e_step, steps, fall, gmat,
    l_pool, l_dico, s_b, r_b, s_p, r_p, s_ec, r_ec, s_ex, r_ex, s_ez, r_ez, s_x, r_x, s_z, r_z, s_a, r_a,
    s_f, r_f, s_g, r_g, s_cx, r_cx, s_cy, r_cy, s_dx, r_dx, s_dy, r_dy, s_cc, r_cc,
):
    y, v = lax.axis_index("frame"), lax.axis_index("vox")
    x, z, c = v // 32, (v // 2) % NZ, v % 2

    def dev(xx, yy, zz, cc):
        return (yy, (xx * NZ + zz) * 2 + cc)

    partner = dev(x, y, z, 1 - c)
    xs = [(x + i) % NX for i in OFFS]
    zs = [(z + o) % NZ for o in FAR]
    xpeer = [dev(xx, y, z, c) for xx in xs]
    xother = [dev(xx, y, z, 1 - c) for xx in xs]
    ypeer = [dev(x, (y + i) % NY, z, c) for i in OFFS]
    zpeer = [dev(x, y, zz, c) for zz in zs[:15]]
    sent = []

    def send(src, dst, ssem, rsem, to):
        copy = pltpu.make_async_remote_copy(
            src_ref=src, dst_ref=dst, send_sem=ssem, recv_sem=rsem, device_id=to, device_id_type=MESH
        )
        copy.start()
        sent.append(copy)
        return copy

    load_pool = pltpu.make_async_copy(pool_in, pool, l_pool)
    load_pool.start()
    load_dico = []
    for j in range(4):
        rows = pl.ds(256 * j, 256)
        load_dico.append(pltpu.make_async_copy(dico_in.at[rows], dico.at[rows], l_dico.at[j]))
        load_dico[j].start()
    barrier = pltpu.get_barrier_semaphore()
    everyone = [partner] + xpeer + xother + ypeer + zpeer
    for to in everyone:
        pl.semaphore_signal(barrier, inc=1, device_id=to, device_id_type=MESH)

    lane = lax.broadcasted_iota(jnp.int32, (128, 128), 1)
    mine = pl.multiple_of(y * 256, 256)
    hot = []
    for r in range(2):
        rows = column(pick[:, 128 * r : 128 * (r + 1)])
        hot.append(jnp.concatenate([(rows == lane + 128 * j).astype(F32).astype(BF) for j in range(4)], axis=1))
    hot = jnp.concatenate(hot, axis=0)
    load_pool.wait()
    batch[pl.ds(mine, 256), :] = jnp.dot(hot, pool[...], preferred_element_type=F32).astype(BF)

    wide = spread()
    for j in range(4):
        rows = slice(256 * j, 256 * (j + 1))
        kept = mm_0(supt[:, rows].astype(F32).astype(BF), wide).astype(BF)
        load_dico[j].wait()
        masked[rows, :] = dico[rows, :] * kept

    def products(half, g, out, kind):
        rows = pl.ds(pl.multiple_of(half * 512, 512), 512)
        right = (batch, masked)[g][pl.ds(mine, 256), :]
        value = mm_t(masked[rows, :], right).astype(kind)
        for xx in range(4):
            for zz in range(16):
                top = xx * 128 + 16 * (zz // 2)
                left = 128 * (zz % 2)
                out[g, xx * 16 + zz] = value[top : top + 16, left : left + 128]

    products(1 - c, 0, psend, BF)
    pl.semaphore_wait(barrier, len(everyone))
    pc = [send(psend.at[0], precv.at[0], s_p.at[0], r_p.at[0], partner)]
    products(1 - c, 1, psend, BF)
    pc.append(send(psend.at[1], precv.at[1], s_p.at[1], r_p.at[1], partner))
    own_batch = batch.at[pl.ds(mine, 256), :]
    b_copies = [send(own_batch, own_batch, s_b.at[k], r_b.at[k], ypeer[k]) for k in range(3)]
    products(c, 0, pown, F32)
    products(c, 1, pown, F32)

    pc[0].wait_recv()
    pc[1].wait_recv()
    xc = []
    for j in range(4):
        for k in range(3):
            for q in range(4):
                t = xs[k] * 16 + zs[4 * j + q]
                for g in range(2):
                    xsend[k, 4 * j + q, g] = (pown[g, t] + precv[g, t].astype(F32)).astype(BF)
            piece = pl.ds(4 * j, 4)
            xc.append(send(xsend.at[k, piece], xrecv.at[k, piece], s_x.at[k, j], r_x.at[k, j], xpeer[k]))

    for j in range(8):
        kept = masked[128 * j : 128 * (j + 1), :].astype(F32)
        part = jnp.zeros((128, 128), F32)
        for b in range(8):
            piece = kept[:, 128 * b : 128 * (b + 1)]
            part += piece * piece
        e_own[j : j + 1, :] = jnp.sum(jnp.transpose(part), axis=0, keepdims=True)
    ec = send(e_own, e_core, s_ec, r_ec, partner)

    zc = []
    for j in range(4):
        for k in range(3):
            xc[3 * j + k].wait_recv()
        for q in range(4):
            n = 4 * j + q
            t = x * 16 + zs[n]
            for g in range(2):
                total = pown[g, t] + precv[g, t].astype(F32)
                for k in range(3):
                    total += xrecv[k, n, g].astype(F32)
                if n < 15:
                    zsend[n, g] = total.astype(BF)
                else:
                    zown[g] = total
            if n < 15:
                zc.append(send(zsend.at[n], zrecv.at[n], s_z.at[n], r_z.at[n], zpeer[n]))
        if j == 0:
            ec.wait_recv()
            e_x[...] = e_own[...] + e_core[...]
            ex = [send(e_x, e_xr.at[k], s_ex.at[k], r_ex.at[k], xpeer[k]) for k in range(3)]
    for k in range(3):
        ex[k].wait_recv()
    e_z[...] = e_x[...] + e_xr[0] + e_xr[1] + e_xr[2]
    ez = [send(e_z, e_zr.at[n], s_ez.at[n], r_ez.at[n], zpeer[n]) for n in range(15)]
    total = zown[...]
    for n in reversed(range(15)):
        zc[n].wait_recv()
        total += zrecv[n].astype(F32)
    zall[15] = total.astype(BF)
    za = [send(zall.at[15], zall.at[n], s_a.at[n], r_a.at[n], zpeer[n]) for n in range(15)]

    for n in reversed(range(15)):
        ez[n].wait_recv()
    energy = e_z[...]
    for n in range(15):
        energy += e_zr[n]
    e_step[...] = 1.0 / (energy + 1e-05)
    block = c * 4 + x
    steps[...] = column(e_step[pl.ds(block, 1), :])

    fc, gc = [], []
    size = 16 // SPLIT
    for j in reversed(range(SPLIT)):
        for n in reversed(range(size * j, size * (j + 1))):
            if n < 15:
                za[n].wait_recv()
            came = (z + NZ - FAR[n]) % NZ
            step = steps[pl.ds(pl.multiple_of(16 * (came // 2), 16), 16), :]
            fall[block, n] = shrink(zall[n, 0].astype(F32) * step, 0.3 * step).astype(BF)
            gmat[y, n] = zall[n, 1]
        piece = pl.ds(size * j, size)
        own_f, own_g = fall.at[block, piece], gmat.at[y, piece]
        for k, to in enumerate(xpeer + xother + [partner]):
            fc.append(send(own_f, own_f, s_f.at[k, j], r_f.at[k, j], to))
        for k in range(3):
            gc.append(send(own_g, own_g, s_g.at[k, j], r_g.at[k, j], ypeer[k]))
    for copy in gc + fc:
        copy.wait_recv()

    def at(row, half):
        o = (z + NZ - 2 * row - half) % NZ
        return jnp.where(o >= 8, 2 * o - 16, 15 - 2 * o)

    def matrix(tiles):
        sides = [jnp.concatenate([tiles(at(row, half)) for row in range(8)], axis=0) for half in range(2)]
        return jnp.concatenate(sides, axis=1)

    push = -matrix(lambda n: zall[n, 0]).astype(F32)
    for g in range(4):
        left = matrix(lambda n: gmat[g, n])
        right = jnp.concatenate([matrix(lambda n: fall[2 * g + b, n]) for b in range(2)], axis=0)
        push += jnp.dot(left, right, preferred_element_type=F32)
    step = jnp.concatenate([steps[...], steps[...]], axis=1)
    first = matrix(lambda n: fall[block, n]).astype(F32)
    codes = shrink(first - step * push, 0.3 * step)
    call[block, pl.ds(mine, 256), :] = jnp.transpose(codes).astype(BF)

    def slot(b, yy, half):
        return call.at[b, pl.ds(pl.multiple_of(yy * 256 + half * 128, 128), 128), :]

    def across(copies, half, over_x):
        ref = slot(block, y, half)
        for k in range(3):
            sems = (s_cx, r_cx) if over_x else (s_cy, r_cy)
            to = xpeer[k] if over_x else ypeer[k]
            copies.append(send(ref, ref, sems[0].at[half, k], sems[1].at[half, k], to))

    x0, x1, y0, y1 = [], [], [], []
    across(x0, 0, True)
    across(y1, 1, False)
    across(x1, 1, True)
    across(y0, 0, False)
    dx, dy = {}, {}
    for k in (1, 2, 0):
        x0[k].wait_recv()
        ref = slot(c * 4 + (x + NX - OFFS[k]) % NX, y, 0)
        for m in range(3):
            dy[k, m] = send(ref, ref, s_dy.at[k, m], r_dy.at[k, m], ypeer[m])
        y1[k].wait_recv()
        ref = slot(block, (y + NY - OFFS[k]) % NY, 1)
        for m in range(3):
            dx[k, m] = send(ref, ref, s_dx.at[k, m], r_dx.at[k, m], xpeer[m])
    cc = []

    def to_partner(yy, half, n):
        ref = call.at[pl.ds(c * 4, 4), pl.ds(pl.multiple_of(yy * 256 + half * 128, 128), 128), :]
        cc.append(send(ref, ref, s_cc.at[n], r_cc.at[n], partner))

    to_partner(y, 0, 0)
    for k in range(3):
        x1[k].wait_recv()
    to_partner(y, 1, 1)
    for m in (1, 2, 0):
        yy = (y + NY - OFFS[m]) % NY
        y0[m].wait_recv()
        for k in range(3):
            dy[k, m].wait_recv()
        to_partner(yy, 0, 2 + 2 * m)
        for k in range(3):
            dx[m, k].wait_recv()
        to_partner(yy, 1, 3 + 2 * m)
    for copy in cc + b_copies:
        copy.wait_recv()
    for copy in sent:
        copy.wait_send()


def finish(call, batch, masked, supt, codes_out, grad_out, own):
    y = lax.axis_index("frame")

    @pl.when(pl.program_id(0) == 0)
    def _():
        rows = pl.ds(pl.multiple_of(y * 256, 256), 256)
        codes_out[...] = jnp.concatenate([call[b, rows, :] for b in range(8)], axis=1)
        for h in range(2):
            own[128 * h : 128 * (h + 1), :] = jnp.transpose(call[2 * y + h])

    total = jnp.zeros((256, 256), F32)
    for half in range(2):
        rows = slice(512 * half, 512 * (half + 1))
        codes = jnp.concatenate([call[b, rows, :] for b in range(8)], axis=1)
        rest = jnp.dot(codes, masked[...], preferred_element_type=F32) - batch[rows, :].astype(F32)
        total += jnp.dot(own[:, rows], rest.astype(BF), preferred_element_type=F32)
    first = pl.program_id(0) * 2
    sup = supt[:, pl.ds(pl.multiple_of(y * 256, 256), 256)].astype(F32).astype(BF)
    place = lax.broadcasted_iota(jnp.int32, (8, 256), 1) // 128 + first
    pick = (place == lax.broadcasted_iota(jnp.int32, (8, 256), 0)).astype(F32).astype(BF)
    grad_out[...] = total * mm_0(sup, pick) * (1.0 / 1024)


def body(pool, dictionary, support, pick):
    dma = pltpu.SemaphoreType.DMA
    sems = [dma(()), dma((4,))]
    for shape in ((3,), (2,), (), (3,), (15,), (3, 4), (15,), (15,), (7, SPLIT), (3, SPLIT), (2, 3), (2, 3), (3, 3), (3, 3), (8,)):
        sems += [dma(shape), dma(shape)]
    vmem = pl.BlockSpec(memory_space=pltpu.VMEM)
    hbm = pl.BlockSpec(memory_space=pltpu.HBM)
    supt = jnp.transpose(support)
    call, batch, masked = pl.pallas_call(
        gather,
        out_shape=(
            jax.ShapeDtypeStruct((8, 1024, 128), BF),
            jax.ShapeDtypeStruct((1024, 1024), BF),
            jax.ShapeDtypeStruct((1024, 1024), BF),
        ),
        in_specs=[hbm, hbm, vmem, vmem],
        out_specs=(vmem, vmem, vmem),
        scratch_shapes=[
            pltpu.VMEM((512, 1024), BF),
            pltpu.VMEM((1024, 1024), BF),
            pltpu.VMEM((2, 64, 16, 128), BF),
            pltpu.VMEM((2, 64, 16, 128), F32),
            pltpu.VMEM((2, 64, 16, 128), BF),
            pltpu.VMEM((3, 16, 2, 16, 128), BF),
            pltpu.VMEM((3, 16, 2, 16, 128), BF),
            pltpu.VMEM((15, 2, 16, 128), BF),
            pltpu.VMEM((15, 2, 16, 128), BF),
            pltpu.VMEM((2, 16, 128), F32),
            pltpu.VMEM((16, 2, 16, 128), BF),
            pltpu.VMEM((8, 128), F32),
            pltpu.VMEM((8, 128), F32),
            pltpu.VMEM((8, 128), F32),
            pltpu.VMEM((3, 8, 128), F32),
            pltpu.VMEM((8, 128), F32),
            pltpu.VMEM((15, 8, 128), F32),
            pltpu.VMEM((8, 128), F32),
            pltpu.VMEM((128, 128), F32),
            pltpu.VMEM((8, 16, 16, 128), BF),
            pltpu.VMEM((4, 16, 16, 128), BF),
        ]
        + sems,
        compiler_params=pltpu.CompilerParams(
            collective_id=0, has_side_effects=True, vmem_limit_bytes=28 * 1024 * 1024
        ),
        cost_estimate=pl.CostEstimate(flops=3 * 10**9, bytes_accessed=6 * 2**20, transcendentals=0),
        name="gather",
    )(pool, dictionary, supt, jnp.reshape(pick, (1, 256)))
    return pl.pallas_call(
        finish,
        grid=(4,),
        out_shape=(jax.ShapeDtypeStruct((256, 1024), BF), jax.ShapeDtypeStruct((256, 1024), F32)),
        in_specs=[
            pl.BlockSpec((8, 1024, 128), lambda n: (0, 0, 0)),
            pl.BlockSpec((1024, 256), lambda n: (0, n)),
            pl.BlockSpec((1024, 256), lambda n: (0, n)),
            pl.BlockSpec((8, 1024), lambda n: (0, 0)),
        ],
        out_specs=(
            pl.BlockSpec((256, 1024), lambda n: (0, 0)),
            pl.BlockSpec((256, 256), lambda n: (0, n)),
        ),
        scratch_shapes=[pltpu.VMEM((256, 1024), BF)],
        compiler_params=pltpu.CompilerParams(vmem_limit_bytes=28 * 1024 * 1024),
        cost_estimate=pl.CostEstimate(flops=3 * 10**9, bytes_accessed=6 * 2**20, transcendentals=0),
        name="finish",
    )(call, batch, masked, supt)


def solution(mesh):
    placed = (P("frame", "vox"), P(None, "vox"), P(None, "vox"), P("frame"))
    return jax.shard_map(
        body,
        mesh=mesh,
        in_specs=placed,
        out_specs=(P("frame", None), P("frame", "vox")),
        check_vma=False,
    )
```

```python
import jax
import jax.numpy as jnp
from jax import lax
from jax.experimental import pallas as pl
from jax.experimental.pallas import tpu as pltpu
from jax.sharding import PartitionSpec as P

MESH = pl.DeviceIdType.MESH
NX, NY, NZ = 4, 4, 16
FAR = (8, 7, 9, 6, 10, 5, 11, 4, 12, 3, 13, 2, 14, 1, 15, 0)
OFFS = (2, 1, 3)
SPLIT = 2
BF, F32 = jnp.bfloat16, jnp.float32


def shrink(value, limit):
    return jnp.where(value < 0, -1.0, 1.0) * jnp.maximum(jnp.abs(value) - limit, 0.0)


def mm_t(left, right):
    return lax.dot_general(left, right, (((1,), (1,)), ((), ())), preferred_element_type=F32)


def mm_0(left, right):
    return lax.dot_general(left, right, (((0,), (0,)), ((), ())), preferred_element_type=F32)


def column(row):
    return jnp.transpose(jnp.broadcast_to(row, (128, 128)))


def spread():
    block_of = lax.broadcasted_iota(jnp.int32, (8, 1024), 1) // 128
    return (block_of == lax.broadcasted_iota(jnp.int32, (8, 1024), 0)).astype(F32).astype(BF)


def gather(
    pool_in, dico_in, supt_in, pick_in, codes_out, total_out,
    pool, dico, supt, pick, call, batch, masked, group_out, total, psend, pown, precv, xsend, xrecv, zsend, zrecv, zown, zall,
    e_own, e_core, e_x, e_xr, e_z, e_zr, e_step, steps, fall, gmat,
    l_pool, l_dico, l_small, l_codes, l_total,
    s_b, r_b, s_p, r_p, s_e, r_e, s_x, r_x, s_z, r_z, s_a, r_a, s_f, r_f, s_g, r_g, s_c, s_cc, r_a0, r_all, r_cc,
):
    y, v = lax.axis_index("frame"), lax.axis_index("vox")
    x, z, c = v // 32, (v // 2) % NZ, v % 2

    def dev(xx, yy, zz, cc):
        return (yy, (xx * NZ + zz) * 2 + cc)

    partner = dev(x, y, z, 1 - c)
    xs = [(x + i) % NX for i in OFFS]
    zs = [(z + o) % NZ for o in FAR]
    xpeer = [dev(xx, y, z, c) for xx in xs]
    xother = [dev(xx, y, z, 1 - c) for xx in xs]
    ypeer = [dev(x, (y + i) % NY, z, c) for i in OFFS]
    zpeer = [dev(x, y, zz, c) for zz in zs[:15]]

    def send(src, dst, ssem, rsem, to):
        pltpu.make_async_remote_copy(
            src_ref=src, dst_ref=dst, send_sem=ssem, recv_sem=rsem, device_id=to, device_id_type=MESH
        ).start()

    def arrived(ref, sem):
        pltpu.make_async_copy(ref, ref, sem).wait()


    load_pick = pltpu.make_async_copy(pick_in, pick, l_small.at[0])
    load_pick.start()
    load_pool = pltpu.make_async_copy(pool_in, pool, l_pool)
    load_pool.start()
    load_supt = pltpu.make_async_copy(supt_in, supt, l_small.at[1])
    load_supt.start()
    load_dico = []
    for j in range(4):
        rows = pl.ds(256 * j, 256)
        load_dico.append(pltpu.make_async_copy(dico_in.at[rows], dico.at[rows], l_dico.at[j]))
        load_dico[j].start()
    barrier = pltpu.get_barrier_semaphore()
    everyone = [partner] + xpeer + xother + ypeer + zpeer
    for to in everyone:
        pl.semaphore_signal(barrier, inc=1, device_id=to, device_id_type=MESH)

    lane = lax.broadcasted_iota(jnp.int32, (128, 128), 1)
    mine = pl.multiple_of(y * 256, 256)
    hot = []
    load_pick.wait()
    for r in range(2):
        rows = column(pick[:, 128 * r : 128 * (r + 1)])
        hot.append(jnp.concatenate([(rows == lane + 128 * j).astype(F32).astype(BF) for j in range(4)], axis=1))
    hot = jnp.concatenate(hot, axis=0)
    load_pool.wait()
    batch[pl.ds(mine, 256), :] = jnp.dot(hot, pool[...], preferred_element_type=F32).astype(BF)

    wide = spread()
    load_supt.wait()
    for j in range(4):
        rows = slice(256 * j, 256 * (j + 1))
        kept = mm_0(supt[:, rows].astype(F32).astype(BF), wide).astype(BF)
        load_dico[j].wait()
        masked[rows, :] = dico[rows, :] * kept

    def products(half, g, out, kind):
        rows = pl.ds(pl.multiple_of(half * 512, 512), 512)
        right = (batch, masked)[g][pl.ds(mine, 256), :]
        value = mm_t(masked[rows, :], right).astype(kind)
        for xx in range(4):
            for zz in range(16):
                top = xx * 128 + 16 * (zz // 2)
                left = 128 * (zz % 2)
                out[g, xx * 16 + zz] = value[top : top + 16, left : left + 128]

    products(1 - c, 0, psend, BF)
    products(1 - c, 1, psend, BF)
    pl.semaphore_wait(barrier, len(everyone))
    send(psend, precv, s_p, r_p, partner)
    own_batch = batch.at[pl.ds(mine, 256), :]
    for k in range(3):
        send(own_batch, own_batch, s_b, r_b.at[k], ypeer[k])
    products(c, 0, pown, F32)
    products(c, 1, pown, F32)

    arrived(precv, r_p)
    for j in range(4):
        for k in range(3):
            for q in range(4):
                t = xs[k] * 16 + zs[4 * j + q]
                for g in range(2):
                    xsend[k, 4 * j + q, g] = (pown[g, t] + precv[g, t].astype(F32)).astype(BF)
            piece = pl.ds(4 * j, 4)
            send(xsend.at[k, piece], xrecv.at[k, piece], s_x, r_x.at[j], xpeer[k])

    for j in range(8):
        kept = masked[128 * j : 128 * (j + 1), :].astype(F32)
        part = jnp.zeros((128, 128), F32)
        for b in range(8):
            piece = kept[:, 128 * b : 128 * (b + 1)]
            part += piece * piece
        e_own[j : j + 1, :] = jnp.sum(jnp.transpose(part), axis=0, keepdims=True)
    send(e_own, e_core, s_e.at[0], r_e.at[0], partner)

    for j in range(4):
        arrived(xrecv.at[:, 4 * j : 4 * j + 4], r_x.at[j])
        for q in range(4):
            n = 4 * j + q
            t = x * 16 + zs[n]
            for g in range(2):
                added = pown[g, t] + precv[g, t].astype(F32)
                for k in range(3):
                    added += xrecv[k, n, g].astype(F32)
                if n < 15:
                    zsend[n, g] = added.astype(BF)
                else:
                    zown[g] = added
            if n < 15:
                send(zsend.at[n], zrecv.at[n], s_z, r_z, zpeer[n])
        if j == 0:
            arrived(e_core, r_e.at[0])
            e_x[...] = e_own[...] + e_core[...]
            for k in range(3):
                send(e_x, e_xr.at[k], s_e.at[1], r_e.at[1], xpeer[k])
    arrived(e_xr, r_e.at[1])
    e_z[...] = e_x[...] + e_xr[0] + e_xr[1] + e_xr[2]
    for n in range(15):
        send(e_z, e_zr.at[n], s_e.at[2], r_e.at[2], zpeer[n])
    arrived(zrecv, r_z)
    added = zown[...]
    for n in range(15):
        added += zrecv[n].astype(F32)
    zall[15] = added.astype(BF)
    size = 16 // SPLIT
    for n in range(15):
        send(zall.at[15], zall.at[n], s_a, r_a.at[n // size], zpeer[n])

    arrived(e_zr, r_e.at[2])
    energy = e_z[...]
    for n in range(15):
        energy += e_zr[n]
    e_step[...] = 1.0 / (energy + 1e-05)
    block = c * 4 + x
    steps[...] = column(e_step[pl.ds(block, 1), :])

    for j in reversed(range(SPLIT)):
        arrived(zall.at[size * j : min(size * (j + 1), 15)], r_a.at[j])
        for n in reversed(range(size * j, size * (j + 1))):
            came = (z + NZ - FAR[n]) % NZ
            step = steps[pl.ds(pl.multiple_of(16 * (came // 2), 16), 16), :]
            fall[block, n] = shrink(zall[n, 0].astype(F32) * step, 0.3 * step).astype(BF)
            gmat[y, n] = zall[n, 1]
        piece = pl.ds(size * j, size)
        own_f, own_g = fall.at[block, piece], gmat.at[y, piece]
        for to in xpeer + xother + [partner]:
            send(own_f, own_f, s_f, r_f, to)
        for k in range(3):
            send(own_g, own_g, s_g, r_g, ypeer[k])
    arrived(fall.at[0:7], r_f)
    arrived(gmat.at[0:3], r_g)

    def at(row, half):
        o = (z + NZ - 2 * row - half) % NZ
        return jnp.where(o >= 8, 2 * o - 16, 15 - 2 * o)

    def matrix(tiles):
        sides = [jnp.concatenate([tiles(at(row, half)) for row in range(8)], axis=0) for half in range(2)]
        return jnp.concatenate(sides, axis=1)

    push = -matrix(lambda n: zall[n, 0]).astype(F32)
    for g in range(4):
        left = matrix(lambda n: gmat[g, n])
        right = jnp.concatenate([matrix(lambda n: fall[2 * g + b, n]) for b in range(2)], axis=0)
        push += jnp.dot(left, right, preferred_element_type=F32)
    step = jnp.concatenate([steps[...], steps[...]], axis=1)
    first = matrix(lambda n: fall[block, n]).astype(F32)
    codes = shrink(first - step * push, 0.3 * step)
    call[block, pl.ds(mine, 256), :] = jnp.transpose(codes).astype(BF)

    def slot(b, yy, half):
        return call.at[b, pl.ds(pl.multiple_of(yy * 256 + half * 128, 128), 128), :]

    def across(half, over_x, sems):
        ref = slot(block, y, half)
        for k in range(3):
            send(ref, ref, s_c, sems[k], (xpeer if over_x else ypeer)[k])

    across(0, True, [r_a0.at[0, k] for k in range(3)])
    across(1, False, [r_a0.at[1, k] for k in range(3)])
    across(1, True, [r_all.at[0, 1]] * 3)
    across(0, False, [r_all.at[1 + k, 0] for k in range(3)])
    third = call.at[0, 0:128, :]
    for k in (1, 2, 0):
        arrived(third, r_a0.at[0, k])
        ref = slot(c * 4 + (x + NX - OFFS[k]) % NX, y, 0)
        for m in range(3):
            send(ref, ref, s_c, r_all.at[1 + m, 0], ypeer[m])
        arrived(third, r_a0.at[1, k])
        ref = slot(block, (y + NY - OFFS[k]) % NY, 1)
        for m in range(3):
            send(ref, ref, s_c, r_all.at[1 + k, 1], xpeer[m])

    def to_partner(yy, half, turn):
        ref = call.at[pl.ds(c * 4, 4), pl.ds(pl.multiple_of(yy * 256 + half * 128, 128), 128), :]
        send(ref, ref, s_cc, r_cc.at[turn], partner)

    def pass_on(turn):
        yy, m = groups[turn]
        if m is None:
            to_partner(yy, 0, turn)
            arrived(call.at[0:3, 0:128, :], r_all.at[0, 1])
            to_partner(yy, 1, turn)
        else:
            arrived(call.at[0:4, 0:128, :], r_all.at[1 + m, 0])
            to_partner(yy, 0, turn)
            arrived(call.at[0:3, 0:128, :], r_all.at[1 + m, 1])
            to_partner(yy, 1, turn)

    def products_of(turn):
        yy, m = groups[turn]
        arrived(call.at[0:4, 0:256, :], r_cc.at[turn])
        if m is not None:
            arrived(own_batch, r_b.at[m])
        rows = pl.ds(pl.multiple_of(yy * 256, 256), 256)
        group = jnp.concatenate([call[b, rows, :] for b in range(8)], axis=1)
        if m is None:
            group_out[...] = group
            write_codes.start()
        own = jnp.concatenate([jnp.transpose(call[2 * y + h, rows, :]) for h in range(2)], axis=0)
        for n in range(2):
            cols = slice(512 * n, 512 * (n + 1))
            rest = jnp.dot(group, masked[:, cols], preferred_element_type=F32) - batch[rows, cols].astype(F32)
            part = jnp.dot(own, rest.astype(BF), preferred_element_type=F32)
            if turn == 0:
                total[:, cols] = part
            else:
                total[:, cols] += part
            if turn == 3:
                write_total[n].start()

    groups = [(y, None)] + [((y + NY - OFFS[m]) % NY, m) for m in (1, 2, 0)]
    write_codes = pltpu.make_async_copy(group_out, codes_out, l_codes)
    write_total = []
    for n in range(2):
        cols = slice(512 * n, 512 * (n + 1))
        write_total.append(pltpu.make_async_copy(total.at[:, cols], total_out.at[:, cols], l_total.at[n]))
    pass_on(0)
    products_of(0)
    pass_on(1)
    pass_on(2)
    products_of(1)
    pass_on(3)
    products_of(2)
    products_of(3)
    write_codes.wait()
    for n in range(2):
        write_total[n].wait()
    for ref, sem in (
        (batch.at[0:768, :], s_b),
        (psend, s_p),
        (e_own, s_e.at[0]),
        (e_xr, s_e.at[1]),
        (e_zr, s_e.at[2]),
        (xsend, s_x),
        (zsend, s_z),
        (zall.at[0:15], s_a),
        (fall.at[0:7], s_f),
        (gmat.at[0:3], s_g),
        (call.at[0:5, 0:768, :], s_c),
        (call.at[0:4], s_cc),
    ):
        arrived(ref, sem)


def finish(codes, total, supt, codes_out, grad_out):
    y = lax.axis_index("frame")
    codes_out[...] = codes[...]
    sup = supt[:, pl.ds(pl.multiple_of(y * 256, 256), 256)].astype(F32).astype(BF)
    first = pl.program_id(0) * 4
    place = lax.broadcasted_iota(jnp.int32, (8, 512), 1) // 128 + first
    pick = (place == lax.broadcasted_iota(jnp.int32, (8, 512), 0)).astype(F32).astype(BF)
    grad_out[...] = total[...] * mm_0(sup, pick) * (1.0 / 1024)


def body(pool, dictionary, support, pick):
    dma = pltpu.SemaphoreType.DMA
    sems = [dma(()), dma((4,)), dma((2,)), dma(()), dma((2,))]
    for shape in ((), (3,), (), (), (3,), (3,), (), (4,), (), (), (), (SPLIT,), (), (), (), (), (), (), (2, 3), (4, 2), (4,)):
        sems.append(dma(shape))
    hbm = pl.BlockSpec(memory_space=pl.ANY)
    supt = jnp.transpose(support)
    codes, total = pl.pallas_call(
        gather,
        out_shape=(jax.ShapeDtypeStruct((256, 1024), BF), jax.ShapeDtypeStruct((256, 1024), F32)),
        in_specs=[hbm] * 4,
        out_specs=(hbm, hbm),
        scratch_shapes=[
            pltpu.VMEM((512, 1024), BF),
            pltpu.VMEM((1024, 1024), BF),
            pltpu.VMEM((8, 1024), jnp.int32),
            pltpu.VMEM((1, 256), jnp.int32),
            pltpu.VMEM((8, 1024, 128), BF),
            pltpu.VMEM((1024, 1024), BF),
            pltpu.VMEM((1024, 1024), BF),
            pltpu.VMEM((256, 1024), BF),
            pltpu.VMEM((256, 1024), F32),
            pltpu.VMEM((2, 64, 16, 128), BF),
            pltpu.VMEM((2, 64, 16, 128), F32),
            pltpu.VMEM((2, 64, 16, 128), BF),
            pltpu.VMEM((3, 16, 2, 16, 128), BF),
            pltpu.VMEM((3, 16, 2, 16, 128), BF),
            pltpu.VMEM((15, 2, 16, 128), BF),
            pltpu.VMEM((15, 2, 16, 128), BF),
            pltpu.VMEM((2, 16, 128), F32),
            pltpu.VMEM((16, 2, 16, 128), BF),
            pltpu.VMEM((8, 128), F32),
            pltpu.VMEM((8, 128), F32),
            pltpu.VMEM((8, 128), F32),
            pltpu.VMEM((3, 8, 128), F32),
            pltpu.VMEM((8, 128), F32),
            pltpu.VMEM((15, 8, 128), F32),
            pltpu.VMEM((8, 128), F32),
            pltpu.VMEM((128, 128), F32),
            pltpu.VMEM((8, 16, 16, 128), BF),
            pltpu.VMEM((4, 16, 16, 128), BF),
        ]
        + sems,
        compiler_params=pltpu.CompilerParams(
            collective_id=0, has_side_effects=True, vmem_limit_bytes=56 * 1024 * 1024
        ),
        cost_estimate=pl.CostEstimate(flops=3 * 10**9, bytes_accessed=6 * 2**20, transcendentals=0),
        name="gather",
    )(pool, dictionary, supt, jnp.reshape(pick, (1, 256)))
    return pl.pallas_call(
        finish,
        grid=(2,),
        out_shape=(jax.ShapeDtypeStruct((256, 1024), BF), jax.ShapeDtypeStruct((256, 1024), F32)),
        in_specs=[
            pl.BlockSpec((256, 512), lambda n: (0, n)),
            pl.BlockSpec((256, 512), lambda n: (0, n)),
            pl.BlockSpec((8, 1024), lambda n: (0, 0)),
        ],
        out_specs=(
            pl.BlockSpec((256, 512), lambda n: (0, n)),
            pl.BlockSpec((256, 512), lambda n: (0, n)),
        ),
        compiler_params=pltpu.CompilerParams(vmem_limit_bytes=56 * 1024 * 1024),
        cost_estimate=pl.CostEstimate(flops=10**7, bytes_accessed=3 * 2**20, transcendentals=0),
        name="finish",
    )(codes, total, supt)


def solution(mesh):
    placed = (P("frame", "vox"), P(None, "vox"), P(None, "vox"), P("frame"))
    return jax.shard_map(
        body,
        mesh=mesh,
        in_specs=placed,
        out_specs=(P("frame", None), P("frame", "vox")),
        check_vma=False,
    )
```

```python
import jax
import jax.numpy as jnp
from jax import lax
from jax.experimental import pallas as pl
from jax.experimental.pallas import tpu as pltpu
from jax.sharding import PartitionSpec as P

MESH = pl.DeviceIdType.MESH
NX, NY, NZ = 4, 4, 16
FAR = (8, 7, 9, 6, 10, 5, 11, 4, 12, 3, 13, 2, 14, 1, 15, 0)
OFFS = (2, 1, 3)
LATE = 4
BF, F32 = jnp.bfloat16, jnp.float32


def shrink(value, limit):
    return jnp.where(value < 0, -1.0, 1.0) * jnp.maximum(jnp.abs(value) - limit, 0.0)


def mm_t(left, right):
    return lax.dot_general(left, right, (((1,), (1,)), ((), ())), preferred_element_type=F32)


def mm_0(left, right):
    return lax.dot_general(left, right, (((0,), (0,)), ((), ())), preferred_element_type=F32)


def column(row):
    return jnp.transpose(jnp.broadcast_to(row, (128, 128)))


def spread():
    block_of = lax.broadcasted_iota(jnp.int32, (8, 1024), 1) // 128
    return (block_of == lax.broadcasted_iota(jnp.int32, (8, 1024), 0)).astype(F32).astype(BF)


def gather(
    pool_in, dico_in, supt_in, pick_in, codes_out, total_out,
    pool, dico, supt, pick, call, batch, masked, group_out, total, psend, pown, precv, xsend, xrecv, zsend, zrecv, zown, zall,
    e_own, e_core, e_x, e_xr, e_z, e_zr, e_step, steps, fall, gmat,
    l_pool, l_dico, l_small, l_codes, l_total,
    s_b, r_b, s_p, r_p, s_e, r_e, s_x, r_x, s_z, r_z, s_a, r_a, s_f, r_f, s_g, r_g, s_c, s_cc, r_a0, r_all, r_cc,
):
    y, v = lax.axis_index("frame"), lax.axis_index("vox")
    x, z, c = v // 32, (v // 2) % NZ, v % 2

    def dev(xx, yy, zz, cc):
        return (yy, (xx * NZ + zz) * 2 + cc)

    partner = dev(x, y, z, 1 - c)
    xs = [(x + i) % NX for i in OFFS]
    zs = [(z + o) % NZ for o in FAR]
    xpeer = [dev(xx, y, z, c) for xx in xs]
    xother = [dev(xx, y, z, 1 - c) for xx in xs]
    ypeer = [dev(x, (y + i) % NY, z, c) for i in OFFS]
    zpeer = [dev(x, y, zz, c) for zz in zs[:15]]

    def send(src, dst, ssem, rsem, to):
        pltpu.make_async_remote_copy(
            src_ref=src, dst_ref=dst, send_sem=ssem, recv_sem=rsem, device_id=to, device_id_type=MESH
        ).start()

    def arrived(ref, sem):
        pltpu.make_async_copy(ref, ref, sem).wait()


    load_pick = pltpu.make_async_copy(pick_in, pick, l_small.at[0])
    load_pick.start()
    load_pool = pltpu.make_async_copy(pool_in, pool, l_pool)
    load_pool.start()
    load_supt = pltpu.make_async_copy(supt_in, supt, l_small.at[1])
    load_supt.start()
    load_dico = []
    for j in range(4):
        rows = pl.ds(256 * j, 256)
        load_dico.append(pltpu.make_async_copy(dico_in.at[rows], dico.at[rows], l_dico.at[j]))
        load_dico[j].start()
    barrier = pltpu.get_barrier_semaphore()
    everyone = [partner] + xpeer + xother + ypeer + zpeer
    for to in everyone:
        pl.semaphore_signal(barrier, inc=1, device_id=to, device_id_type=MESH)

    lane = lax.broadcasted_iota(jnp.int32, (128, 128), 1)
    mine = pl.multiple_of(y * 256, 256)
    hot = []
    load_pick.wait()
    for r in range(2):
        rows = column(pick[:, 128 * r : 128 * (r + 1)])
        hot.append(jnp.concatenate([(rows == lane + 128 * j).astype(F32).astype(BF) for j in range(4)], axis=1))
    hot = jnp.concatenate(hot, axis=0)
    load_pool.wait()
    batch[pl.ds(mine, 256), :] = jnp.dot(hot, pool[...], preferred_element_type=F32).astype(BF)

    wide = spread()
    load_supt.wait()
    for j in range(4):
        rows = slice(256 * j, 256 * (j + 1))
        kept = mm_0(supt[:, rows].astype(F32).astype(BF), wide).astype(BF)
        load_dico[j].wait()
        masked[rows, :] = dico[rows, :] * kept

    def products(half, g, out, kind):
        rows = pl.ds(pl.multiple_of(half * 512, 512), 512)
        right = (batch, masked)[g][pl.ds(mine, 256), :]
        value = mm_t(masked[rows, :], right).astype(kind)
        for xx in range(4):
            for zz in range(16):
                top = xx * 128 + 16 * (zz // 2)
                left = 128 * (zz % 2)
                out[g, xx * 16 + zz] = value[top : top + 16, left : left + 128]

    products(1 - c, 0, psend, BF)
    pl.semaphore_wait(barrier, len(everyone))
    send(psend.at[0], precv.at[0], s_p, r_p.at[0], partner)
    products(1 - c, 1, psend, BF)
    send(psend.at[1], precv.at[1], s_p, r_p.at[1], partner)
    own_batch = batch.at[pl.ds(mine, 256), :]
    for k in range(3):
        send(own_batch, own_batch, s_b, r_b.at[k], ypeer[k])

    for g in range(2):
        products(c, g, pown, F32)
        arrived(precv.at[g], r_p.at[g])
        for j in range(2):
            piece = pl.ds(8 * j, 8)
            for k in range(3):
                for n in range(8 * j, 8 * j + 8):
                    t = xs[k] * 16 + zs[n]
                    xsend[k, g, n] = (pown[g, t] + precv[g, t].astype(F32)).astype(BF)
                send(xsend.at[k, g, piece], xrecv.at[k, g, piece], s_x, r_x.at[g, j], xpeer[k])

    for j in range(8):
        kept = masked[128 * j : 128 * (j + 1), :].astype(F32)
        part = jnp.zeros((128, 128), F32)
        for b in range(8):
            piece = kept[:, 128 * b : 128 * (b + 1)]
            part += piece * piece
        e_own[j : j + 1, :] = jnp.sum(jnp.transpose(part), axis=0, keepdims=True)
    send(e_own, e_core, s_e.at[0], r_e.at[0], partner)

    for g in range(2):
        for j in range(2):
            arrived(xrecv.at[:, g, 8 * j : 8 * j + 8], r_x.at[g, j])
            for n in range(8 * j, 8 * j + 8):
                t = x * 16 + zs[n]
                added = pown[g, t] + precv[g, t].astype(F32)
                for k in range(3):
                    added += xrecv[k, g, n].astype(F32)
                if n < 15:
                    zsend[g, n] = added.astype(BF)
                    send(zsend.at[g, n], zrecv.at[g, n], s_z, r_z.at[g], zpeer[n])
                else:
                    zown[g] = added
        if g == 0:
            arrived(e_core, r_e.at[0])
            e_x[...] = e_own[...] + e_core[...]
            for k in range(3):
                send(e_x, e_xr.at[k], s_e.at[1], r_e.at[1], xpeer[k])
    arrived(e_xr, r_e.at[1])
    e_z[...] = e_x[...] + e_xr[0] + e_xr[1] + e_xr[2]
    for n in range(15):
        send(e_z, e_zr.at[n], s_e.at[2], r_e.at[2], zpeer[n])
    for g in range(2):
        arrived(zrecv.at[g], r_z.at[g])
        added = zown[g]
        for n in range(15):
            added += zrecv[g, n].astype(F32)
        zall[g, 15] = added.astype(BF)
        for n in range(15):
            send(zall.at[g, 15], zall.at[g, n], s_a, r_a.at[g, int(n >= LATE)], zpeer[n])

    arrived(e_zr, r_e.at[2])
    energy = e_z[...]
    for n in range(15):
        energy += e_zr[n]
    e_step[...] = 1.0 / (energy + 1e-05)
    block = c * 4 + x
    steps[...] = column(e_step[pl.ds(block, 1), :])

    for j in (1, 0):
        low, high = (LATE, 16) if j else (0, LATE)
        slots = range(low, high)
        piece = pl.ds(low, high - low)
        arrived(zall.at[0, low : high - j], r_a.at[0, j])
        for n in slots:
            came = (z + NZ - FAR[n]) % NZ
            step = steps[pl.ds(pl.multiple_of(16 * (came // 2), 16), 16), :]
            fall[block, n] = shrink(zall[0, n].astype(F32) * step, 0.3 * step).astype(BF)
        ref = fall.at[block, piece]
        for to in xpeer + xother + [partner]:
            send(ref, ref, s_f, r_f, to)
        arrived(zall.at[1, low : high - j], r_a.at[1, j])
        for n in slots:
            gmat[y, n] = zall[1, n]
        ref = gmat.at[y, piece]
        for k in range(3):
            send(ref, ref, s_g, r_g, ypeer[k])
    arrived(fall.at[0:7], r_f)
    arrived(gmat.at[0:3], r_g)

    def at(row, half):
        o = (z + NZ - 2 * row - half) % NZ
        return jnp.where(o >= 8, 2 * o - 16, 15 - 2 * o)

    def matrix(tiles):
        sides = [jnp.concatenate([tiles(at(row, half)) for row in range(8)], axis=0) for half in range(2)]
        return jnp.concatenate(sides, axis=1)

    push = -matrix(lambda n: zall[0, n]).astype(F32)
    for g in range(4):
        left = matrix(lambda n: gmat[g, n])
        right = jnp.concatenate([matrix(lambda n: fall[2 * g + b, n]) for b in range(2)], axis=0)
        push += jnp.dot(left, right, preferred_element_type=F32)
    step = jnp.concatenate([steps[...], steps[...]], axis=1)
    first = matrix(lambda n: fall[block, n]).astype(F32)
    codes = shrink(first - step * push, 0.3 * step)
    call[block, pl.ds(mine, 256), :] = jnp.transpose(codes).astype(BF)

    def slot(b, yy, half):
        return call.at[b, pl.ds(pl.multiple_of(yy * 256 + half * 128, 128), 128), :]

    def across(half, over_x, sems):
        ref = slot(block, y, half)
        for k in range(3):
            send(ref, ref, s_c, sems[k], (xpeer if over_x else ypeer)[k])

    across(0, True, [r_a0.at[0, k] for k in range(3)])
    across(1, False, [r_a0.at[1, k] for k in range(3)])
    across(1, True, [r_all.at[0, 1]] * 3)
    across(0, False, [r_all.at[1 + k, 0] for k in range(3)])
    third = call.at[0, 0:128, :]
    for k in (1, 2, 0):
        arrived(third, r_a0.at[0, k])
        ref = slot(c * 4 + (x + NX - OFFS[k]) % NX, y, 0)
        for m in range(3):
            send(ref, ref, s_c, r_all.at[1 + m, 0], ypeer[m])
        arrived(third, r_a0.at[1, k])
        ref = slot(block, (y + NY - OFFS[k]) % NY, 1)
        for m in range(3):
            send(ref, ref, s_c, r_all.at[1 + k, 1], xpeer[m])

    def to_partner(yy, half, turn):
        ref = call.at[pl.ds(c * 4, 4), pl.ds(pl.multiple_of(yy * 256 + half * 128, 128), 128), :]
        send(ref, ref, s_cc, r_cc.at[turn], partner)

    def pass_on(turn):
        yy, m = groups[turn]
        if m is None:
            to_partner(yy, 0, turn)
            arrived(call.at[0:3, 0:128, :], r_all.at[0, 1])
            to_partner(yy, 1, turn)
        else:
            arrived(call.at[0:4, 0:128, :], r_all.at[1 + m, 0])
            to_partner(yy, 0, turn)
            arrived(call.at[0:3, 0:128, :], r_all.at[1 + m, 1])
            to_partner(yy, 1, turn)

    def products_of(turn):
        yy, m = groups[turn]
        arrived(call.at[0:4, 0:256, :], r_cc.at[turn])
        if m is not None:
            arrived(own_batch, r_b.at[m])
        rows = pl.ds(pl.multiple_of(yy * 256, 256), 256)
        group = jnp.concatenate([call[b, rows, :] for b in range(8)], axis=1)
        if m is None:
            group_out[...] = group
            write_codes.start()
        own = jnp.concatenate([jnp.transpose(call[2 * y + h, rows, :]) for h in range(2)], axis=0)
        for n in range(2):
            cols = slice(512 * n, 512 * (n + 1))
            rest = jnp.dot(group, masked[:, cols], preferred_element_type=F32) - batch[rows, cols].astype(F32)
            part = jnp.dot(own, rest.astype(BF), preferred_element_type=F32)
            if turn == 0:
                total[:, cols] = part
            else:
                total[:, cols] += part
            if turn == 3:
                write_total[n].start()

    groups = [(y, None)] + [((y + NY - OFFS[m]) % NY, m) for m in (1, 2, 0)]
    write_codes = pltpu.make_async_copy(group_out, codes_out, l_codes)
    write_total = []
    for n in range(2):
        cols = slice(512 * n, 512 * (n + 1))
        write_total.append(pltpu.make_async_copy(total.at[:, cols], total_out.at[:, cols], l_total.at[n]))
    pass_on(0)
    products_of(0)
    pass_on(1)
    pass_on(2)
    products_of(1)
    pass_on(3)
    products_of(2)
    products_of(3)
    write_codes.wait()
    for n in range(2):
        write_total[n].wait()
    for ref, sem in (
        (batch.at[0:768, :], s_b),
        (psend, s_p),
        (e_own, s_e.at[0]),
        (e_xr, s_e.at[1]),
        (e_zr, s_e.at[2]),
        (xsend, s_x),
        (zsend, s_z),
        (zall.at[:, 0:15], s_a),
        (fall.at[0:7], s_f),
        (gmat.at[0:3], s_g),
        (call.at[0:5, 0:768, :], s_c),
        (call.at[0:4], s_cc),
    ):
        arrived(ref, sem)


def finish(codes, total, supt, codes_out, grad_out):
    y = lax.axis_index("frame")
    codes_out[...] = codes[...]
    sup = supt[:, pl.ds(pl.multiple_of(y * 256, 256), 256)].astype(F32).astype(BF)
    first = pl.program_id(0) * 4
    place = lax.broadcasted_iota(jnp.int32, (8, 512), 1) // 128 + first
    pick = (place == lax.broadcasted_iota(jnp.int32, (8, 512), 0)).astype(F32).astype(BF)
    grad_out[...] = total[...] * mm_0(sup, pick) * (1.0 / 1024)


def body(pool, dictionary, support, pick):
    dma = pltpu.SemaphoreType.DMA
    sems = [dma(()), dma((4,)), dma((2,)), dma(()), dma((2,))]
    for shape in ((), (3,), (), (2,), (3,), (3,), (), (2, 2), (), (2,), (), (2, 2), (), (), (), (), (), (), (2, 3), (4, 2), (4,)):
        sems.append(dma(shape))
    hbm = pl.BlockSpec(memory_space=pl.ANY)
    supt = jnp.transpose(support)
    codes, total = pl.pallas_call(
        gather,
        out_shape=(jax.ShapeDtypeStruct((256, 1024), BF), jax.ShapeDtypeStruct((256, 1024), F32)),
        in_specs=[hbm] * 4,
        out_specs=(hbm, hbm),
        scratch_shapes=[
            pltpu.VMEM((512, 1024), BF),
            pltpu.VMEM((1024, 1024), BF),
            pltpu.VMEM((8, 1024), jnp.int32),
            pltpu.VMEM((1, 256), jnp.int32),
            pltpu.VMEM((8, 1024, 128), BF),
            pltpu.VMEM((1024, 1024), BF),
            pltpu.VMEM((1024, 1024), BF),
            pltpu.VMEM((256, 1024), BF),
            pltpu.VMEM((256, 1024), F32),
            pltpu.VMEM((2, 64, 16, 128), BF),
            pltpu.VMEM((2, 64, 16, 128), F32),
            pltpu.VMEM((2, 64, 16, 128), BF),
            pltpu.VMEM((3, 2, 16, 16, 128), BF),
            pltpu.VMEM((3, 2, 16, 16, 128), BF),
            pltpu.VMEM((2, 15, 16, 128), BF),
            pltpu.VMEM((2, 15, 16, 128), BF),
            pltpu.VMEM((2, 16, 128), F32),
            pltpu.VMEM((2, 16, 16, 128), BF),
            pltpu.VMEM((8, 128), F32),
            pltpu.VMEM((8, 128), F32),
            pltpu.VMEM((8, 128), F32),
            pltpu.VMEM((3, 8, 128), F32),
            pltpu.VMEM((8, 128), F32),
            pltpu.VMEM((15, 8, 128), F32),
            pltpu.VMEM((8, 128), F32),
            pltpu.VMEM((128, 128), F32),
            pltpu.VMEM((8, 16, 16, 128), BF),
            pltpu.VMEM((4, 16, 16, 128), BF),
        ]
        + sems,
        compiler_params=pltpu.CompilerParams(
            collective_id=0, has_side_effects=True, vmem_limit_bytes=56 * 1024 * 1024
        ),
        cost_estimate=pl.CostEstimate(flops=3 * 10**9, bytes_accessed=6 * 2**20, transcendentals=0),
        name="gather",
    )(pool, dictionary, supt, jnp.reshape(pick, (1, 256)))
    return pl.pallas_call(
        finish,
        grid=(2,),
        out_shape=(jax.ShapeDtypeStruct((256, 1024), BF), jax.ShapeDtypeStruct((256, 1024), F32)),
        in_specs=[
            pl.BlockSpec((256, 512), lambda n: (0, n)),
            pl.BlockSpec((256, 512), lambda n: (0, n)),
            pl.BlockSpec((8, 1024), lambda n: (0, 0)),
        ],
        out_specs=(
            pl.BlockSpec((256, 512), lambda n: (0, n)),
            pl.BlockSpec((256, 512), lambda n: (0, n)),
        ),
        compiler_params=pltpu.CompilerParams(vmem_limit_bytes=56 * 1024 * 1024),
        cost_estimate=pl.CostEstimate(flops=10**7, bytes_accessed=3 * 2**20, transcendentals=0),
        name="finish",
    )(codes, total, supt)


def solution(mesh):
    placed = (P("frame", "vox"), P(None, "vox"), P(None, "vox"), P("frame"))
    return jax.shard_map(
        body,
        mesh=mesh,
        in_specs=placed,
        out_specs=(P("frame", None), P("frame", "vox")),
        check_vma=False,
    )
```

```python
import jax
import jax.numpy as jnp
from jax import lax
from jax.experimental import pallas as pl
from jax.experimental.pallas import tpu as pltpu
from jax.sharding import PartitionSpec as P

MESH = pl.DeviceIdType.MESH
NX, NY, NZ = 4, 4, 16
FAR = (8, 7, 9, 6, 10, 5, 11, 4, 12, 3, 13, 2, 14, 1, 15, 0)
OFFS = (2, 1, 3)
LATE = 4
BF, F32 = jnp.bfloat16, jnp.float32


def shrink(value, limit):
    return jnp.where(value < 0, -1.0, 1.0) * jnp.maximum(jnp.abs(value) - limit, 0.0)


def mm_t(left, right):
    return lax.dot_general(left, right, (((1,), (1,)), ((), ())), preferred_element_type=F32)


def mm_0(left, right):
    return lax.dot_general(left, right, (((0,), (0,)), ((), ())), preferred_element_type=F32)


def column(row):
    return jnp.transpose(jnp.broadcast_to(row, (128, 128)))


def spread():
    block_of = lax.broadcasted_iota(jnp.int32, (8, 1024), 1) // 128
    return (block_of == lax.broadcasted_iota(jnp.int32, (8, 1024), 0)).astype(F32).astype(BF)


def gather(
    pool_in, dico_in, supt_in, pick_in, codes_out, total_out,
    pool, dico, supt, pick, call, batch, masked, group_out, total, psend, pown, precv, xsend, xrecv, zsend, zrecv, zown, zall,
    e_own, e_core, e_x, e_xr, e_z, e_zr, steps, fall, gmat,
    l_pool, l_dico, l_small, l_codes, l_total,
    s_b, r_b, s_p, r_p, s_e, r_e, s_x, r_x, s_z, r_z, s_a, r_a, s_f, r_f, s_g, r_g, s_c, s_cc, r_a0, r_all, r_cc,
):
    y, v = lax.axis_index("frame"), lax.axis_index("vox")
    x, z, c = v // 32, (v // 2) % NZ, v % 2

    def dev(xx, yy, zz, cc):
        return (yy, (xx * NZ + zz) * 2 + cc)

    partner = dev(x, y, z, 1 - c)
    xs = [(x + i) % NX for i in OFFS]
    zs = [(z + o) % NZ for o in FAR]
    xpeer = [dev(xx, y, z, c) for xx in xs]
    xother = [dev(xx, y, z, 1 - c) for xx in xs]
    ypeer = [dev(x, (y + i) % NY, z, c) for i in OFFS]
    zpeer = [dev(x, y, zz, c) for zz in zs[:15]]

    def send(src, dst, ssem, rsem, to):
        pltpu.make_async_remote_copy(
            src_ref=src, dst_ref=dst, send_sem=ssem, recv_sem=rsem, device_id=to, device_id_type=MESH
        ).start()

    def arrived(ref, sem):
        pltpu.make_async_copy(ref, ref, sem).wait()


    load_pick = pltpu.make_async_copy(pick_in, pick, l_small.at[0])
    load_pick.start()
    load_pool = pltpu.make_async_copy(pool_in, pool, l_pool)
    load_pool.start()
    load_supt = pltpu.make_async_copy(supt_in, supt, l_small.at[1])
    load_supt.start()
    load_dico = []
    for j in range(4):
        rows = pl.ds(256 * j, 256)
        load_dico.append(pltpu.make_async_copy(dico_in.at[rows], dico.at[rows], l_dico.at[j]))
        load_dico[j].start()
    barrier = pltpu.get_barrier_semaphore()
    everyone = [partner] + xpeer + xother + ypeer + zpeer
    for to in everyone:
        pl.semaphore_signal(barrier, inc=1, device_id=to, device_id_type=MESH)

    lane = lax.broadcasted_iota(jnp.int32, (128, 128), 1)
    mine = pl.multiple_of(y * 256, 256)
    hot = []
    load_pick.wait()
    for r in range(2):
        rows = column(pick[:, 128 * r : 128 * (r + 1)])
        hot.append(jnp.concatenate([(rows == lane + 128 * j).astype(F32).astype(BF) for j in range(4)], axis=1))
    hot = jnp.concatenate(hot, axis=0)
    load_pool.wait()
    batch[pl.ds(mine, 256), :] = jnp.dot(hot, pool[...], preferred_element_type=F32).astype(BF)

    wide = spread()
    load_supt.wait()
    for j in range(4):
        rows = slice(256 * j, 256 * (j + 1))
        kept = mm_0(supt[:, rows].astype(F32).astype(BF), wide).astype(BF)
        load_dico[j].wait()
        masked[rows, :] = dico[rows, :] * kept

    def products(half, g, out, kind):
        rows = pl.ds(pl.multiple_of(half * 512, 512), 512)
        right = (batch, masked)[g][pl.ds(mine, 256), :]
        value = mm_t(masked[rows, :], right).astype(kind)
        for xx in range(4):
            for zz in range(16):
                top = xx * 128 + 16 * (zz // 2)
                left = 128 * (zz % 2)
                out[g, xx * 16 + zz] = value[top : top + 16, left : left + 128]

    products(1 - c, 0, psend, BF)
    pl.semaphore_wait(barrier, len(everyone))
    send(psend.at[0], precv.at[0], s_p, r_p.at[0], partner)
    products(1 - c, 1, psend, BF)
    send(psend.at[1], precv.at[1], s_p, r_p.at[1], partner)
    own_batch = batch.at[pl.ds(mine, 256), :]
    for k in range(3):
        send(own_batch, own_batch, s_b, r_b.at[k], ypeer[k])

    for g in range(2):
        products(c, g, pown, F32)
        arrived(precv.at[g], r_p.at[g])
        for j in range(2):
            piece = pl.ds(8 * j, 8)
            for k in range(3):
                for n in range(8 * j, 8 * j + 8):
                    t = xs[k] * 16 + zs[n]
                    xsend[k, g, n] = (pown[g, t] + precv[g, t].astype(F32)).astype(BF)
                send(xsend.at[k, g, piece], xrecv.at[k, g, piece], s_x, r_x.at[g, j], xpeer[k])

    for j in range(8):
        kept = masked[128 * j : 128 * (j + 1), :].astype(F32)
        part = jnp.zeros((128, 128), F32)
        for b in range(8):
            piece = kept[:, 128 * b : 128 * (b + 1)]
            part += piece * piece
        e_own[j] = jnp.sum(jnp.transpose(part), axis=0, keepdims=True)
    send(e_own.at[pl.ds((1 - c) * 4, 4)], e_core, s_e.at[0], r_e.at[0], partner)

    for g in range(2):
        for j in range(2):
            arrived(xrecv.at[:, g, 8 * j : 8 * j + 8], r_x.at[g, j])
            for n in range(8 * j, 8 * j + 8):
                t = x * 16 + zs[n]
                added = pown[g, t] + precv[g, t].astype(F32)
                for k in range(3):
                    added += xrecv[k, g, n].astype(F32)
                if n < 15:
                    zsend[g, n] = added.astype(BF)
                    send(zsend.at[g, n], zrecv.at[g, n], s_z, r_z.at[g], zpeer[n])
                else:
                    zown[g] = added
        if g == 0:
            arrived(e_core, r_e.at[0])
            e_x[...] = e_own[pl.ds(c * 4, 4)] + e_core[...]
            for k in range(3):
                send(e_x.at[xs[k]], e_xr.at[k], s_e.at[1], r_e.at[1], xpeer[k])
    arrived(e_xr, r_e.at[1])
    e_z[...] = e_x[x] + e_xr[0] + e_xr[1] + e_xr[2]
    for n in range(15):
        send(e_z, e_zr.at[n], s_e.at[2], r_e.at[2], zpeer[n])
    for g in range(2):
        arrived(zrecv.at[g], r_z.at[g])
        added = zown[g]
        for n in range(15):
            added += zrecv[g, n].astype(F32)
        zall[g, 15] = added.astype(BF)
        for n in range(15):
            send(zall.at[g, 15], zall.at[g, n], s_a, r_a.at[g, int(n >= LATE)], zpeer[n])

    arrived(e_zr, r_e.at[2])
    energy = e_z[...]
    for n in range(15):
        energy += e_zr[n]
    block = c * 4 + x
    steps[...] = column(1.0 / (energy + 1e-05))

    for j in (1, 0):
        low, high = (LATE, 16) if j else (0, LATE)
        slots = range(low, high)
        piece = pl.ds(low, high - low)
        arrived(zall.at[0, low : high - j], r_a.at[0, j])
        for n in slots:
            came = (z + NZ - FAR[n]) % NZ
            step = steps[pl.ds(pl.multiple_of(16 * (came // 2), 16), 16), :]
            fall[block, n] = shrink(zall[0, n].astype(F32) * step, 0.3 * step).astype(BF)
        ref = fall.at[block, piece]
        for to in xpeer + xother + [partner]:
            send(ref, ref, s_f, r_f, to)
        arrived(zall.at[1, low : high - j], r_a.at[1, j])
        for n in slots:
            gmat[y, n] = zall[1, n]
        ref = gmat.at[y, piece]
        for k in range(3):
            send(ref, ref, s_g, r_g, ypeer[k])
    arrived(fall.at[0:7], r_f)
    arrived(gmat.at[0:3], r_g)

    def at(row, half):
        o = (z + NZ - 2 * row - half) % NZ
        return jnp.where(o >= 8, 2 * o - 16, 15 - 2 * o)

    def matrix(tiles):
        sides = [jnp.concatenate([tiles(at(row, half)) for row in range(8)], axis=0) for half in range(2)]
        return jnp.concatenate(sides, axis=1)

    push = -matrix(lambda n: zall[0, n]).astype(F32)
    for g in range(4):
        left = matrix(lambda n: gmat[g, n])
        right = jnp.concatenate([matrix(lambda n: fall[2 * g + b, n]) for b in range(2)], axis=0)
        push += jnp.dot(left, right, preferred_element_type=F32)
    step = jnp.concatenate([steps[...], steps[...]], axis=1)
    first = matrix(lambda n: fall[block, n]).astype(F32)
    codes = shrink(first - step * push, 0.3 * step)
    call[block, pl.ds(mine, 256), :] = jnp.transpose(codes).astype(BF)

    def slot(b, yy, half):
        return call.at[b, pl.ds(pl.multiple_of(yy * 256 + half * 128, 128), 128), :]

    def across(half, over_x, sems):
        ref = slot(block, y, half)
        for k in range(3):
            send(ref, ref, s_c, sems[k], (xpeer if over_x else ypeer)[k])

    across(0, True, [r_a0.at[0, k] for k in range(3)])
    across(1, False, [r_a0.at[1, k] for k in range(3)])
    across(1, True, [r_all.at[0, 1]] * 3)
    across(0, False, [r_all.at[1 + k, 0] for k in range(3)])
    third = call.at[0, 0:128, :]
    for k in (1, 2, 0):
        arrived(third, r_a0.at[0, k])
        ref = slot(c * 4 + (x + NX - OFFS[k]) % NX, y, 0)
        for m in range(3):
            send(ref, ref, s_c, r_all.at[1 + m, 0], ypeer[m])
        arrived(third, r_a0.at[1, k])
        ref = slot(block, (y + NY - OFFS[k]) % NY, 1)
        for m in range(3):
            send(ref, ref, s_c, r_all.at[1 + k, 1], xpeer[m])

    def to_partner(yy, half, turn):
        ref = call.at[pl.ds(c * 4, 4), pl.ds(pl.multiple_of(yy * 256 + half * 128, 128), 128), :]
        send(ref, ref, s_cc, r_cc.at[turn], partner)

    def pass_on(turn):
        yy, m = groups[turn]
        if m is None:
            to_partner(yy, 0, turn)
            arrived(call.at[0:3, 0:128, :], r_all.at[0, 1])
            to_partner(yy, 1, turn)
        else:
            arrived(call.at[0:4, 0:128, :], r_all.at[1 + m, 0])
            to_partner(yy, 0, turn)
            arrived(call.at[0:3, 0:128, :], r_all.at[1 + m, 1])
            to_partner(yy, 1, turn)

    def products_of(turn):
        yy, m = groups[turn]
        arrived(call.at[0:4, 0:256, :], r_cc.at[turn])
        if m is not None:
            arrived(own_batch, r_b.at[m])
        rows = pl.ds(pl.multiple_of(yy * 256, 256), 256)
        group = jnp.concatenate([call[b, rows, :] for b in range(8)], axis=1)
        if m is None:
            group_out[...] = group
            write_codes.start()
        own = jnp.concatenate([jnp.transpose(call[2 * y + h, rows, :]) for h in range(2)], axis=0)
        for n in range(2):
            cols = slice(512 * n, 512 * (n + 1))
            rest = jnp.dot(group, masked[:, cols], preferred_element_type=F32) - batch[rows, cols].astype(F32)
            part = jnp.dot(own, rest.astype(BF), preferred_element_type=F32)
            if turn == 0:
                total[:, cols] = part
            else:
                total[:, cols] += part
            if turn == 3:
                write_total[n].start()

    groups = [(y, None)] + [((y + NY - OFFS[m]) % NY, m) for m in (1, 2, 0)]
    write_codes = pltpu.make_async_copy(group_out, codes_out, l_codes)
    write_total = []
    for n in range(2):
        cols = slice(512 * n, 512 * (n + 1))
        write_total.append(pltpu.make_async_copy(total.at[:, cols], total_out.at[:, cols], l_total.at[n]))
    pass_on(0)
    products_of(0)
    pass_on(1)
    pass_on(2)
    products_of(1)
    pass_on(3)
    products_of(2)
    products_of(3)
    write_codes.wait()
    for n in range(2):
        write_total[n].wait()
    for ref, sem in (
        (batch.at[0:768, :], s_b),
        (psend, s_p),
        (e_core, s_e.at[0]),
        (e_xr, s_e.at[1]),
        (e_zr, s_e.at[2]),
        (xsend, s_x),
        (zsend, s_z),
        (zall.at[:, 0:15], s_a),
        (fall.at[0:7], s_f),
        (gmat.at[0:3], s_g),
        (call.at[0:5, 0:768, :], s_c),
        (call.at[0:4], s_cc),
    ):
        arrived(ref, sem)


def finish(codes, total, supt, codes_out, grad_out):
    y = lax.axis_index("frame")
    codes_out[...] = codes[...]
    sup = supt[:, pl.ds(pl.multiple_of(y * 256, 256), 256)].astype(F32).astype(BF)
    first = pl.program_id(0) * 4
    place = lax.broadcasted_iota(jnp.int32, (8, 512), 1) // 128 + first
    pick = (place == lax.broadcasted_iota(jnp.int32, (8, 512), 0)).astype(F32).astype(BF)
    grad_out[...] = total[...] * mm_0(sup, pick) * (1.0 / 1024)


def body(pool, dictionary, support, pick):
    dma = pltpu.SemaphoreType.DMA
    sems = [dma(()), dma((4,)), dma((2,)), dma(()), dma((2,))]
    for shape in ((), (3,), (), (2,), (3,), (3,), (), (2, 2), (), (2,), (), (2, 2), (), (), (), (), (), (), (2, 3), (4, 2), (4,)):
        sems.append(dma(shape))
    hbm = pl.BlockSpec(memory_space=pl.ANY)
    supt = jnp.transpose(support)
    codes, total = pl.pallas_call(
        gather,
        out_shape=(jax.ShapeDtypeStruct((256, 1024), BF), jax.ShapeDtypeStruct((256, 1024), F32)),
        in_specs=[hbm] * 4,
        out_specs=(hbm, hbm),
        scratch_shapes=[
            pltpu.VMEM((512, 1024), BF),
            pltpu.VMEM((1024, 1024), BF),
            pltpu.VMEM((8, 1024), jnp.int32),
            pltpu.VMEM((1, 256), jnp.int32),
            pltpu.VMEM((8, 1024, 128), BF),
            pltpu.VMEM((1024, 1024), BF),
            pltpu.VMEM((1024, 1024), BF),
            pltpu.VMEM((256, 1024), BF),
            pltpu.VMEM((256, 1024), F32),
            pltpu.VMEM((2, 64, 16, 128), BF),
            pltpu.VMEM((2, 64, 16, 128), F32),
            pltpu.VMEM((2, 64, 16, 128), BF),
            pltpu.VMEM((3, 2, 16, 16, 128), BF),
            pltpu.VMEM((3, 2, 16, 16, 128), BF),
            pltpu.VMEM((2, 15, 16, 128), BF),
            pltpu.VMEM((2, 15, 16, 128), BF),
            pltpu.VMEM((2, 16, 128), F32),
            pltpu.VMEM((2, 16, 16, 128), BF),
            pltpu.VMEM((8, 1, 128), F32),
            pltpu.VMEM((4, 1, 128), F32),
            pltpu.VMEM((4, 1, 128), F32),
            pltpu.VMEM((3, 1, 128), F32),
            pltpu.VMEM((1, 128), F32),
            pltpu.VMEM((15, 1, 128), F32),
            pltpu.VMEM((128, 128), F32),
            pltpu.VMEM((8, 16, 16, 128), BF),
            pltpu.VMEM((4, 16, 16, 128), BF),
        ]
        + sems,
        compiler_params=pltpu.CompilerParams(
            collective_id=0, has_side_effects=True, vmem_limit_bytes=56 * 1024 * 1024
        ),
        cost_estimate=pl.CostEstimate(flops=3 * 10**9, bytes_accessed=6 * 2**20, transcendentals=0),
        name="gather",
    )(pool, dictionary, supt, jnp.reshape(pick, (1, 256)))
    return pl.pallas_call(
        finish,
        grid=(2,),
        out_shape=(jax.ShapeDtypeStruct((256, 1024), BF), jax.ShapeDtypeStruct((256, 1024), F32)),
        in_specs=[
            pl.BlockSpec((256, 512), lambda n: (0, n)),
            pl.BlockSpec((256, 512), lambda n: (0, n)),
            pl.BlockSpec((8, 1024), lambda n: (0, 0)),
        ],
        out_specs=(
            pl.BlockSpec((256, 512), lambda n: (0, n)),
            pl.BlockSpec((256, 512), lambda n: (0, n)),
        ),
        compiler_params=pltpu.CompilerParams(vmem_limit_bytes=56 * 1024 * 1024),
        cost_estimate=pl.CostEstimate(flops=10**7, bytes_accessed=3 * 2**20, transcendentals=0),
        name="finish",
    )(codes, total, supt)


def solution(mesh):
    placed = (P("frame", "vox"), P(None, "vox"), P(None, "vox"), P("frame"))
    return jax.shard_map(
        body,
        mesh=mesh,
        in_specs=placed,
        out_specs=(P("frame", None), P("frame", "vox")),
        check_vma=False,
    )
```

```python
import jax
import jax.numpy as jnp
from jax import lax
from jax.experimental import pallas as pl
from jax.experimental.pallas import tpu as pltpu
from jax.sharding import PartitionSpec as P

MESH = pl.DeviceIdType.MESH
NX, NY, NZ = 4, 4, 16
FAR = (8, 7, 9, 6, 10, 5, 11, 4, 12, 3, 13, 2, 14, 1, 15, 0)
OFFS = (2, 1, 3)
LATE = 4
BF, F32 = jnp.bfloat16, jnp.float32


def shrink(value, limit):
    return jnp.where(value < 0, -1.0, 1.0) * jnp.maximum(jnp.abs(value) - limit, 0.0)


def mm_t(left, right):
    return lax.dot_general(left, right, (((1,), (1,)), ((), ())), preferred_element_type=F32)


def mm_0(left, right):
    return lax.dot_general(left, right, (((0,), (0,)), ((), ())), preferred_element_type=F32)


def column(row):
    return jnp.transpose(jnp.broadcast_to(row, (128, 128)))


def spread():
    block_of = lax.broadcasted_iota(jnp.int32, (8, 1024), 1) // 128
    return (block_of == lax.broadcasted_iota(jnp.int32, (8, 1024), 0)).astype(F32).astype(BF)


def gather(
    pool_in, dico_in, supt_in, pick_in, codes_out, total_out,
    pool, dico, supt, pick, call, batch, masked, group_out, total, psend, pown, precv, xsend, xrecv, zsend, zrecv, zown, zall,
    e_own, e_core, e_x, e_xr, e_z, e_zr, steps, fall, gmat,
    l_pool, l_dico, l_small, l_codes, l_total,
    s_b, r_b, s_p, r_p, s_e, r_e, s_x, r_x, s_z, r_z, s_a, r_a, s_f, r_f, s_fc, r_fc, s_g, r_g, s_c, s_cc, r_a0, r_all, r_cc,
):
    y, v = lax.axis_index("frame"), lax.axis_index("vox")
    x, z, c = v // 32, (v // 2) % NZ, v % 2

    def dev(xx, yy, zz, cc):
        return (yy, (xx * NZ + zz) * 2 + cc)

    partner = dev(x, y, z, 1 - c)
    xs = [(x + i) % NX for i in OFFS]
    zs = [(z + o) % NZ for o in FAR]
    xpeer = [dev(xx, y, z, c) for xx in xs]
    ypeer = [dev(x, (y + i) % NY, z, c) for i in OFFS]
    zpeer = [dev(x, y, zz, c) for zz in zs[:15]]

    def send(src, dst, ssem, rsem, to):
        pltpu.make_async_remote_copy(
            src_ref=src, dst_ref=dst, send_sem=ssem, recv_sem=rsem, device_id=to, device_id_type=MESH
        ).start()

    def arrived(ref, sem):
        pltpu.make_async_copy(ref, ref, sem).wait()


    load_pick = pltpu.make_async_copy(pick_in, pick, l_small.at[0])
    load_pick.start()
    load_pool = pltpu.make_async_copy(pool_in, pool, l_pool)
    load_pool.start()
    load_supt = pltpu.make_async_copy(supt_in, supt, l_small.at[1])
    load_supt.start()
    load_dico = []
    for j in range(4):
        rows = pl.ds(256 * j, 256)
        load_dico.append(pltpu.make_async_copy(dico_in.at[rows], dico.at[rows], l_dico.at[j]))
        load_dico[j].start()
    barrier = pltpu.get_barrier_semaphore()
    everyone = zpeer + xpeer + ypeer + [partner]
    for to in everyone:
        pl.semaphore_signal(barrier, inc=1, device_id=to, device_id_type=MESH)

    lane = lax.broadcasted_iota(jnp.int32, (128, 128), 1)
    mine = pl.multiple_of(y * 256, 256)
    hot = []
    load_pick.wait()
    for r in range(2):
        rows = column(pick[:, 128 * r : 128 * (r + 1)])
        hot.append(jnp.concatenate([(rows == lane + 128 * j).astype(F32).astype(BF) for j in range(4)], axis=1))
    hot = jnp.concatenate(hot, axis=0)
    load_pool.wait()
    batch[pl.ds(mine, 256), :] = jnp.dot(hot, pool[...], preferred_element_type=F32).astype(BF)

    wide = spread()
    load_supt.wait()
    for j in range(4):
        rows = slice(256 * j, 256 * (j + 1))
        kept = mm_0(supt[:, rows].astype(F32).astype(BF), wide).astype(BF)
        load_dico[j].wait()
        masked[rows, :] = dico[rows, :] * kept

    def products(half, g, out, kind):
        rows = pl.ds(pl.multiple_of(half * 512, 512), 512)
        right = (batch, masked)[g][pl.ds(mine, 256), :]
        value = mm_t(masked[rows, :], right).astype(kind)
        for xx in range(4):
            for zz in range(16):
                top = xx * 128 + 16 * (zz // 2)
                left = 128 * (zz % 2)
                out[g, xx * 16 + zz] = value[top : top + 16, left : left + 128]

    for g in range(2):
        products(1 - c, g, psend, BF)
    pl.semaphore_wait(barrier, len(everyone))
    for g in range(2):
        send(psend.at[g], precv.at[g], s_p, r_p.at[g], partner)
    own_batch = batch.at[pl.ds(mine, 256), :]
    for k in range(3):
        send(own_batch, own_batch, s_b, r_b.at[k], ypeer[k])

    for g in range(2):
        products(c, g, pown, F32)
        arrived(precv.at[g], r_p.at[g])
        for j in range(2):
            piece = pl.ds(8 * j, 8)
            for k in range(3):
                for n in range(8 * j, 8 * j + 8):
                    t = xs[k] * 16 + zs[n]
                    xsend[k, g, n] = (pown[g, t] + precv[g, t].astype(F32)).astype(BF)
                send(xsend.at[k, g, piece], xrecv.at[k, g, piece], s_x, r_x.at[g, j], xpeer[k])

    for j in range(8):
        kept = masked[128 * j : 128 * (j + 1), :].astype(F32)
        part = jnp.zeros((128, 128), F32)
        for b in range(8):
            piece = kept[:, 128 * b : 128 * (b + 1)]
            part += piece * piece
        e_own[j] = jnp.sum(jnp.transpose(part), axis=0, keepdims=True)
    send(e_own.at[pl.ds((1 - c) * 4, 4)], e_core, s_e.at[0], r_e.at[0], partner)

    for g in range(2):
        for j in range(2):
            arrived(xrecv.at[:, g, 8 * j : 8 * j + 8], r_x.at[g, j])
            for n in range(8 * j, 8 * j + 8):
                t = x * 16 + zs[n]
                added = pown[g, t] + precv[g, t].astype(F32)
                for k in range(3):
                    added += xrecv[k, g, n].astype(F32)
                if n < 15:
                    zsend[g, n] = added.astype(BF)
                    send(zsend.at[g, n], zrecv.at[g, n], s_z, r_z.at[g], zpeer[n])
                else:
                    zown[g] = added
        if g == 0:
            arrived(e_core, r_e.at[0])
            e_x[...] = e_own[pl.ds(c * 4, 4)] + e_core[...]
            for k in range(3):
                send(e_x.at[xs[k]], e_xr.at[k], s_e.at[1], r_e.at[1], xpeer[k])
    arrived(e_xr, r_e.at[1])
    e_z[...] = e_x[x] + e_xr[0] + e_xr[1] + e_xr[2]
    for n in range(15):
        send(e_z, e_zr.at[n], s_e.at[2], r_e.at[2], zpeer[n])
    for g in range(2):
        arrived(zrecv.at[g], r_z.at[g])
        added = zown[g]
        for n in range(15):
            added += zrecv[g, n].astype(F32)
        zall[g, 15] = added.astype(BF)
        for n in range(15):
            send(zall.at[g, 15], zall.at[g, n], s_a, r_a.at[g, int(n >= LATE)], zpeer[n])

    arrived(e_zr, r_e.at[2])
    energy = e_z[...]
    for n in range(15):
        energy += e_zr[n]
    block = c * 4 + x
    steps[...] = column(1.0 / (energy + 1e-05))

    def swap(j):
        low, high = (LATE, 16) if j else (0, LATE)
        piece = pl.ds(low, high - low)
        arrived(fall.at[0:3, piece], r_f.at[j])
        ref = fall.at[pl.ds(c * 4, 4), piece]
        send(ref, ref, s_fc, r_fc.at[j], partner)

    for j in (1, 0):
        low, high = (LATE, 16) if j else (0, LATE)
        slots = range(low, high)
        piece = pl.ds(low, high - low)
        for g in range(2):
            arrived(zall.at[g, low : high - j], r_a.at[g, j])
            if g == 0:
                for n in slots:
                    came = (z + NZ - FAR[n]) % NZ
                    step = steps[pl.ds(pl.multiple_of(16 * (came // 2), 16), 16), :]
                    fall[block, n] = shrink(zall[0, n].astype(F32) * step, 0.3 * step).astype(BF)
                ref = fall.at[block, piece]
                for to in xpeer:
                    send(ref, ref, s_f, r_f.at[j], to)
                if j == 0:
                    swap(1)
            else:
                for n in slots:
                    gmat[y, n] = zall[1, n]
                ref = gmat.at[y, piece]
                for k in range(3):
                    send(ref, ref, s_g, r_g, ypeer[k])
    swap(0)
    arrived(fall.at[0:4, LATE:16], r_fc.at[1])
    arrived(fall.at[0:4, 0:LATE], r_fc.at[0])
    arrived(gmat.at[0:3], r_g)

    def at(row, half):
        o = (z + NZ - 2 * row - half) % NZ
        return jnp.where(o >= 8, 2 * o - 16, 15 - 2 * o)

    def matrix(tiles):
        sides = [jnp.concatenate([tiles(at(row, half)) for row in range(8)], axis=0) for half in range(2)]
        return jnp.concatenate(sides, axis=1)

    push = -matrix(lambda n: zall[0, n]).astype(F32)
    for g in range(4):
        left = matrix(lambda n: gmat[g, n])
        right = jnp.concatenate([matrix(lambda n: fall[2 * g + b, n]) for b in range(2)], axis=0)
        push += jnp.dot(left, right, preferred_element_type=F32)
    step = jnp.concatenate([steps[...], steps[...]], axis=1)
    first = matrix(lambda n: fall[block, n]).astype(F32)
    codes = shrink(first - step * push, 0.3 * step)
    call[block, pl.ds(mine, 256), :] = jnp.transpose(codes).astype(BF)

    def slot(b, yy, half):
        return call.at[b, pl.ds(pl.multiple_of(yy * 256 + half * 128, 128), 128), :]

    def across(half, over_x, sems):
        ref = slot(block, y, half)
        for k in range(3):
            send(ref, ref, s_c, sems[k], (xpeer if over_x else ypeer)[k])

    across(0, True, [r_a0.at[0, k] for k in range(3)])
    across(1, False, [r_a0.at[1, k] for k in range(3)])
    across(1, True, [r_all.at[0, 1]] * 3)
    across(0, False, [r_all.at[1 + k, 0] for k in range(3)])
    third = call.at[0, 0:128, :]
    for k in (1, 2, 0):
        arrived(third, r_a0.at[0, k])
        ref = slot(c * 4 + (x + NX - OFFS[k]) % NX, y, 0)
        for m in range(3):
            send(ref, ref, s_c, r_all.at[1 + m, 0], ypeer[m])
        arrived(third, r_a0.at[1, k])
        ref = slot(block, (y + NY - OFFS[k]) % NY, 1)
        for m in range(3):
            send(ref, ref, s_c, r_all.at[1 + k, 1], xpeer[m])

    def to_partner(yy, half, turn):
        ref = call.at[pl.ds(c * 4, 4), pl.ds(pl.multiple_of(yy * 256 + half * 128, 128), 128), :]
        send(ref, ref, s_cc, r_cc.at[turn], partner)

    def pass_on(turn):
        yy, m = groups[turn]
        if m is None:
            to_partner(yy, 0, turn)
            arrived(call.at[0:3, 0:128, :], r_all.at[0, 1])
            to_partner(yy, 1, turn)
        else:
            arrived(call.at[0:4, 0:128, :], r_all.at[1 + m, 0])
            to_partner(yy, 0, turn)
            arrived(call.at[0:3, 0:128, :], r_all.at[1 + m, 1])
            to_partner(yy, 1, turn)

    def products_of(turn):
        yy, m = groups[turn]
        arrived(call.at[0:4, 0:256, :], r_cc.at[turn])
        if m is not None:
            arrived(own_batch, r_b.at[m])
        rows = pl.ds(pl.multiple_of(yy * 256, 256), 256)
        group = jnp.concatenate([call[b, rows, :] for b in range(8)], axis=1)
        if m is None:
            group_out[...] = group
            write_codes.start()
        own = jnp.concatenate([jnp.transpose(call[2 * y + h, rows, :]) for h in range(2)], axis=0)
        for n in range(2):
            cols = slice(512 * n, 512 * (n + 1))
            rest = jnp.dot(group, masked[:, cols], preferred_element_type=F32) - batch[rows, cols].astype(F32)
            part = jnp.dot(own, rest.astype(BF), preferred_element_type=F32)
            if turn == 0:
                total[:, cols] = part
            else:
                total[:, cols] += part
            if turn == 3:
                write_total[n].start()

    groups = [(y, None)] + [((y + NY - OFFS[m]) % NY, m) for m in (1, 2, 0)]
    write_codes = pltpu.make_async_copy(group_out, codes_out, l_codes)
    write_total = []
    for n in range(2):
        cols = slice(512 * n, 512 * (n + 1))
        write_total.append(pltpu.make_async_copy(total.at[:, cols], total_out.at[:, cols], l_total.at[n]))
    pass_on(0)
    products_of(0)
    pass_on(1)
    pass_on(2)
    products_of(1)
    pass_on(3)
    products_of(2)
    products_of(3)
    write_codes.wait()
    for n in range(2):
        write_total[n].wait()
    for ref, sem in (
        (batch.at[0:768, :], s_b),
        (psend, s_p),
        (e_core, s_e.at[0]),
        (e_xr, s_e.at[1]),
        (e_zr, s_e.at[2]),
        (xsend, s_x),
        (zsend, s_z),
        (zall.at[:, 0:15], s_a),
        (fall.at[0:3], s_f),
        (fall.at[0:4], s_fc),
        (gmat.at[0:3], s_g),
        (call.at[0:5, 0:768, :], s_c),
        (call.at[0:4], s_cc),
    ):
        arrived(ref, sem)


def finish(codes, total, supt, codes_out, grad_out):
    y = lax.axis_index("frame")
    codes_out[...] = codes[...]
    sup = supt[:, pl.ds(pl.multiple_of(y * 256, 256), 256)].astype(F32).astype(BF)
    first = pl.program_id(0) * 4
    place = lax.broadcasted_iota(jnp.int32, (8, 512), 1) // 128 + first
    pick = (place == lax.broadcasted_iota(jnp.int32, (8, 512), 0)).astype(F32).astype(BF)
    grad_out[...] = total[...] * mm_0(sup, pick) * (1.0 / 1024)


def body(pool, dictionary, support, pick):
    dma = pltpu.SemaphoreType.DMA
    sems = [dma(()), dma((4,)), dma((2,)), dma(()), dma((2,))]
    for shape in ((), (3,), (), (2,), (3,), (3,), (), (2, 2), (), (2,), (), (2, 2), (), (2,), (), (2,), (), (), (), (), (2, 3), (4, 2), (4,)):
        sems.append(dma(shape))
    hbm = pl.BlockSpec(memory_space=pl.ANY)
    supt = jnp.transpose(support)
    codes, total = pl.pallas_call(
        gather,
        out_shape=(jax.ShapeDtypeStruct((256, 1024), BF), jax.ShapeDtypeStruct((256, 1024), F32)),
        in_specs=[hbm] * 4,
        out_specs=(hbm, hbm),
        scratch_shapes=[
            pltpu.VMEM((512, 1024), BF),
            pltpu.VMEM((1024, 1024), BF),
            pltpu.VMEM((8, 1024), jnp.int32),
            pltpu.VMEM((1, 256), jnp.int32),
            pltpu.VMEM((8, 1024, 128), BF),
            pltpu.VMEM((1024, 1024), BF),
            pltpu.VMEM((1024, 1024), BF),
            pltpu.VMEM((256, 1024), BF),
            pltpu.VMEM((256, 1024), F32),
            pltpu.VMEM((2, 64, 16, 128), BF),
            pltpu.VMEM((2, 64, 16, 128), F32),
            pltpu.VMEM((2, 64, 16, 128), BF),
            pltpu.VMEM((3, 2, 16, 16, 128), BF),
            pltpu.VMEM((3, 2, 16, 16, 128), BF),
            pltpu.VMEM((2, 15, 16, 128), BF),
            pltpu.VMEM((2, 15, 16, 128), BF),
            pltpu.VMEM((2, 16, 128), F32),
            pltpu.VMEM((2, 16, 16, 128), BF),
            pltpu.VMEM((8, 1, 128), F32),
            pltpu.VMEM((4, 1, 128), F32),
            pltpu.VMEM((4, 1, 128), F32),
            pltpu.VMEM((3, 1, 128), F32),
            pltpu.VMEM((1, 128), F32),
            pltpu.VMEM((15, 1, 128), F32),
            pltpu.VMEM((128, 128), F32),
            pltpu.VMEM((8, 16, 16, 128), BF),
            pltpu.VMEM((4, 16, 16, 128), BF),
        ]
        + sems,
        compiler_params=pltpu.CompilerParams(
            collective_id=0, has_side_effects=True, vmem_limit_bytes=56 * 1024 * 1024
        ),
        cost_estimate=pl.CostEstimate(flops=3 * 10**9, bytes_accessed=6 * 2**20, transcendentals=0),
        name="gather",
    )(pool, dictionary, supt, jnp.reshape(pick, (1, 256)))
    return pl.pallas_call(
        finish,
        grid=(2,),
        out_shape=(jax.ShapeDtypeStruct((256, 1024), BF), jax.ShapeDtypeStruct((256, 1024), F32)),
        in_specs=[
            pl.BlockSpec((256, 512), lambda n: (0, n)),
            pl.BlockSpec((256, 512), lambda n: (0, n)),
            pl.BlockSpec((8, 1024), lambda n: (0, 0)),
        ],
        out_specs=(
            pl.BlockSpec((256, 512), lambda n: (0, n)),
            pl.BlockSpec((256, 512), lambda n: (0, n)),
        ),
        compiler_params=pltpu.CompilerParams(vmem_limit_bytes=56 * 1024 * 1024),
        cost_estimate=pl.CostEstimate(flops=10**7, bytes_accessed=3 * 2**20, transcendentals=0),
        name="finish",
    )(codes, total, supt)


def solution(mesh):
    placed = (P("frame", "vox"), P(None, "vox"), P(None, "vox"), P("frame"))
    return jax.shard_map(
        body,
        mesh=mesh,
        in_specs=placed,
        out_specs=(P("frame", None), P("frame", "vox")),
        check_vma=False,
    )
```
